32 devices in a mesh: ctx: 16 (over z, x, core), fsdp: 2 (over y).
Axes of the slice: x: 2, y: 2, z: 4, core: 2. Of those that a mesh axis runs over, the one named last changes fastest.
Arguments:
- inputs: bfloat16 [2, 2, 2048, 768], P(None, 'fsdp', 'ctx'), may hold values from -6 to 6
- cotangent: bfloat16 [2, 2, 2048, 768], P(None, 'fsdp', 'ctx'), may hold values from -6 to 6
- lengths: int32 [2, 2], P(None, 'fsdp'), may hold values from 512 to 2048, as said below
- ln1_gain: bfloat16 [768], P('fsdp'), may hold values from 0.5 to 1.5
- ln1_bias: bfloat16 [768], P('fsdp'), may hold values from -1.75 to 1.75
- w_qkv: bfloat16 [768, 2304], P('fsdp'), may hold values from -0.21875 to 0.21875
- bias_q: bfloat16 [768], P('fsdp'), may hold values from -1.75 to 1.75
- bias_v: bfloat16 [768], P('fsdp'), may hold values from -1.75 to 1.75
- w_out: bfloat16 [768, 768], P('fsdp'), may hold values from -2.5 to 2.5
- bias_out: bfloat16 [768], P('fsdp'), may hold values from -1.75 to 1.75
- ln2_gain: bfloat16 [768], P('fsdp'), may hold values from 0.5 to 1.5
- ln2_bias: bfloat16 [768], P('fsdp'), may hold values from -1.75 to 1.75
- w_up: bfloat16 [768, 3072], P('fsdp'), may hold values from -0.21875 to 0.21875
- bias_up: bfloat16 [3072], P('fsdp'), may hold values from -1.75 to 1.75
- w_down: bfloat16 [3072, 768], P('fsdp'), may hold values from -0.109375 to 0.109375
- bias_down: bfloat16 [768], P('fsdp'), may hold values from -1.75 to 1.75
Outputs:
- outputs: bfloat16 [2, 2, 2048, 768], P(None, 'fsdp', 'ctx')
- grad_inputs: bfloat16 [2, 2, 2048, 768], P(None, 'fsdp', 'ctx')
- grad_ln1_gain: float32 [768], P('fsdp')
- grad_ln1_bias: float32 [768], P('fsdp')
- grad_w_qkv: float32 [768, 2304], P('fsdp')
- grad_bias_q: float32 [768], P('fsdp')
- grad_bias_v: float32 [768], P('fsdp')
- grad_w_out: float32 [768, 768], P('fsdp')
- grad_bias_out: float32 [768], P('fsdp')
- grad_ln2_gain: float32 [768], P('fsdp')
- grad_ln2_bias: float32 [768], P('fsdp')
- grad_w_up: float32 [768, 3072], P('fsdp')
- grad_bias_up: float32 [3072], P('fsdp')
- grad_w_down: float32 [3072, 768], P('fsdp')
- grad_bias_down: float32 [768], P('fsdp')
The draws below stay inside these ranges and needn't reach their ends.
Inputs may be any that keep to these rules, and one draw needn't show every extreme that they name: For each of the 2 sequence places, one of the 2 micro-batches, drawn from the seed, has length 2048; the other lengths are drawn evenly.
All inputs are finite; a program needn't handle non-finite values.
Results may differ from the reference program's by a relative error of at most 0.023.
Values may be sent and summed in bfloat16 or wider, within the bound.
A program may use at most 320 MiB of HBM per device.

```python
import math
import jax
import jax.numpy as jnp
from jax import lax

D = 768
HEADS = 12
HDIM = 64
FF = 3072
MB = 2
SEQ = 2048
SEQS = 2


def draw_lengths(key, part):
    spread = jax.random.randint(key, (MB, SEQS), SEQ // 4, SEQ + 1)
    chosen = jax.random.randint(jax.random.fold_in(key, 7), (SEQS,), 0, MB)
    return jnp.where(jnp.arange(MB)[:, None] == chosen[None, :], SEQ, spread).astype(jnp.int32)


def block_levels(key, shape, shards, low, top_value):
    level = 1.0
    for position, blocks in shards:
        draws = jax.random.uniform(jax.random.fold_in(jax.random.fold_in(key, 6), position), (blocks,), jnp.float32, low / len(shards), top_value / len(shards))
        level = level * jnp.repeat(jnp.exp(draws), shape[position] // blocks).reshape((-1,) + (1,) * (len(shape) - 1 - position))
    return level


def bell_draw(rng, shape, width, most, cuts=(), held_as=jnp.bfloat16):
    values = width * jax.random.normal(rng, shape, jnp.float32)
    if cuts:
        values = values * block_levels(rng, shape, cuts, -0.22, 0.18)
    return jnp.clip(values, -most, most).astype(held_as)


def setup_inputs(seed: int = 0) -> dict:
    arg_keys = jax.random.split(jax.random.key(seed), 17)
    inputs = bell_draw(arg_keys[0], (MB, SEQS, SEQ, D), 1.0, 6.0, ((1, 2), (2, 16)))
    cotangent = bell_draw(arg_keys[1], (MB, SEQS, SEQ, D), 1.0, 6.0, ((1, 2), (2, 16)))
    lengths = draw_lengths(jax.random.fold_in(arg_keys[16], 71), 0)
    ln1_gain = jnp.clip(1.0 + 0.1 * jax.random.normal(arg_keys[3], (D,), jnp.float32), 0.5, 1.5).astype(jnp.bfloat16)
    ln1_bias = bell_draw(arg_keys[4], (D,), 0.3, 1.75, ((0, 2),))
    w_qkv = bell_draw(arg_keys[5], (D, 3 * D), D ** -0.5, 0.21875, ((0, 2),))
    bias_q = bell_draw(arg_keys[6], (D,), 0.3, 1.75, ((0, 2),))
    bias_v = bell_draw(arg_keys[7], (D,), 0.3, 1.75, ((0, 2),))
    w_out = bell_draw(arg_keys[8], (D, D), (max(1, D * 16 // SEQ)) ** -0.5, 2.5, ((0, 2),))
    bias_out = bell_draw(arg_keys[9], (D,), 0.3, 1.75, ((0, 2),))
    ln2_gain = jnp.clip(1.0 + 0.1 * jax.random.normal(arg_keys[10], (D,), jnp.float32), 0.5, 1.5).astype(jnp.bfloat16)
    ln2_bias = bell_draw(arg_keys[11], (D,), 0.3, 1.75, ((0, 2),))
    w_up = bell_draw(arg_keys[12], (D, FF), D ** -0.5, 0.21875, ((0, 2),))
    bias_up = bell_draw(arg_keys[13], (FF,), 0.3, 1.75, ((0, 2),))
    w_down = bell_draw(arg_keys[14], (FF, D), FF ** -0.5, 0.109375, ((0, 2),))
    bias_down = bell_draw(arg_keys[15], (D,), 0.3, 1.75, ((0, 2),))
    return {"inputs": inputs, "cotangent": cotangent, "lengths": lengths, "ln1_gain": ln1_gain, "ln1_bias": ln1_bias, "w_qkv": w_qkv, "bias_q": bias_q, "bias_v": bias_v, "w_out": w_out, "bias_out": bias_out, "ln2_gain": ln2_gain, "ln2_bias": ln2_bias, "w_up": w_up, "bias_up": bias_up, "w_down": w_down, "bias_down": bias_down}


@jax.custom_vjp
def low(v):
    return lax.optimization_barrier(v.astype(jnp.bfloat16)).astype(jnp.float32)

@jax.custom_vjp
def low_back(v):
    return v

def low_keep(v):
    return (low(v), None)

def low_pass(kept, grad):
    return (grad,)

def back_keep(v):
    return (v, None)

def back_low(kept, grad):
    return (low(grad),)
low.defvjp(low_keep, low_pass)
low_back.defvjp(back_keep, back_low)
epsilon = 1e-06
highest = lax.Precision.HIGHEST

def layer_norm(values, scaling, offset):
    row_mean = lax.optimization_barrier(jnp.mean(values, axis=-1, keepdims=True))
    centred = values - row_mean
    variance = lax.optimization_barrier(jnp.mean(centred * centred, axis=-1, keepdims=True))
    return centred * lax.rsqrt(variance + epsilon) * scaling + offset

def attention_block(query_block, key_heads, value_heads, key_live):
    raw_scores = jnp.einsum('qhd,khd->hqk', query_block, key_heads, precision=highest)
    scores = low_back(raw_scores) * HDIM ** (-0.5)
    scores = jnp.where(key_live[None, None, :], scores, -1e+30)
    top_score = lax.optimization_barrier(jnp.max(scores, axis=-1, keepdims=True))
    expanded = jnp.where(key_live[None, None, :], jnp.exp(scores - top_score), 0.0)
    probability = expanded / lax.optimization_barrier(jnp.sum(expanded, axis=-1, keepdims=True))
    return jnp.einsum('hqk,khd->qhd', low(probability), value_heads, precision=highest)

def layer_forward(params, source, length):
    first_scale, first_shift, joint_weight, query_shift, value_shift, output_weight, output_shift, second_scale, second_shift, upward_weight, upward_shift, downward_weight, downward_shift = params
    first_low = low(layer_norm(source, first_scale, first_shift))
    shifts = jnp.concatenate([query_shift, jnp.zeros_like(query_shift), value_shift])
    joint_rows = jnp.dot(first_low, joint_weight, precision=highest) + shifts
    joint_rows = low(low_back(joint_rows))
    query_heads = joint_rows[:, :D].reshape(SEQ, HEADS, HDIM)
    key_heads = joint_rows[:, D:2 * D].reshape(SEQ, HEADS, HDIM)
    value_heads = joint_rows[:, 2 * D:].reshape(SEQ, HEADS, HDIM)
    key_live = jnp.arange(SEQ) < length
    block_rows = math.gcd(SEQ, 512)
    query_blocks = query_heads.reshape(SEQ // block_rows, block_rows, HEADS, HDIM)

    def attend_block(query_block):
        return attention_block(query_block, key_heads, value_heads, key_live)
    mixed = lax.map(jax.checkpoint(attend_block), query_blocks)
    mixed = low(low_back(mixed.reshape(SEQ, D)))
    branch = low_back(jnp.dot(mixed, output_weight, precision=highest) + output_shift)
    residual = source + branch
    second_low = low(layer_norm(residual, second_scale, second_shift))
    upper = low_back(jnp.dot(second_low, upward_weight, precision=highest) + upward_shift)
    active = low(jax.nn.gelu(upper, approximate=False))
    return residual + jnp.dot(active, downward_weight, precision=highest) + downward_shift

def reference(inputs, cotangent, lengths, ln1_gain, ln1_bias, w_qkv, bias_q, bias_v, w_out, bias_out, ln2_gain, ln2_bias, w_up, bias_up, w_down, bias_down):
    params = tuple((member.astype(jnp.float32) for member in (ln1_gain, ln1_bias, w_qkv, bias_q, bias_v, w_out, bias_out, ln2_gain, ln2_bias, w_up, bias_up, w_down, bias_down)))
    flat_in = inputs.astype(jnp.float32).reshape(MB * SEQS, SEQ, D)
    flat_cot = cotangent.astype(jnp.float32).reshape(MB * SEQS, SEQ, D)
    flat_len = lengths.reshape(MB * SEQS).astype(jnp.int32)

    def one_sequence(totals, packed):
        seq_in, seq_cot, seq_len = packed

        def forward(weights, source):
            return layer_forward(weights, source, seq_len)
        result, pullback = jax.vjp(forward, params, seq_in)
        live_rows = (jnp.arange(SEQ) < seq_len)[:, None]
        grad_w, grad_in = pullback(jnp.where(live_rows, seq_cot, 0.0))
        totals = jax.tree.map(jnp.add, totals, grad_w)
        return (totals, (result.astype(jnp.bfloat16), grad_in.astype(jnp.bfloat16)))
    zero_grads = jax.tree.map(jnp.zeros_like, params)
    totals, stacked = lax.scan(one_sequence, zero_grads, (flat_in, flat_cot, flat_len))
    outputs = stacked[0].reshape(MB, SEQS, SEQ, D)
    grad_inputs = stacked[1].reshape(MB, SEQS, SEQ, D)
    return (outputs, grad_inputs, totals[0], totals[1], totals[2], totals[3], totals[4], totals[5], totals[6], totals[7], totals[8], totals[9], totals[10], totals[11], totals[12])
```

```python
import functools
import heapq

import jax
import jax.numpy as jnp
from jax import lax
from jax.experimental import pallas as pl
from jax.experimental.pallas import tpu as pltpu
from jax.sharding import PartitionSpec as P

HEADS = 12
HDIM = 64
GROUPS = 8
EPS = 1e-6
BF = jnp.bfloat16
F32 = jnp.float32
WIDE = 512
MESH = pl.DeviceIdType.MESH


def dot_nn(a, b):
    return lax.dot_general(a, b, (((1,), (0,)), ((), ())), preferred_element_type=F32)


def dot_nt(a, b):
    return lax.dot_general(a, b, (((1,), (1,)), ((), ())), preferred_element_type=F32)


def dot_tn(a, b):
    return lax.dot_general(a, b, (((0,), (0,)), ((), ())), preferred_element_type=F32)


def flip(index, bit):
    return index + bit - 2 * bit * ((index // bit) % 2)


def span(start, size, unit=16):
    return pl.ds(pl.multiple_of(start, unit), size)


class Copy:
    def __init__(self, wire, src, dst, ctx, fsdp, landing):
        self.wire, self.src, self.dst, self.landing = wire, src, dst, landing
        self.ctx, self.fsdp, self.i = ctx, fsdp, wire.count
        self.arrived = False
        wire.count += 1

    def of(self, dst):
        return pltpu.make_async_remote_copy(
            src_ref=self.src, dst_ref=dst, send_sem=self.wire.send.at[self.i], recv_sem=self.wire.recv.at[self.i],
            device_id=(self.ctx, self.fsdp), device_id_type=MESH,
        )

    def start(self):
        self.of(self.dst).start()
        self.wire.open.append(self)
        return self

    def arrive(self):
        self.of(self.landing).wait_recv()
        self.arrived = True

    def left(self):
        self.of(self.dst).wait_send()


class Wire:
    def __init__(self, send, recv, fsdp):
        self.send, self.recv, self.fsdp = send, recv, fsdp
        self.count, self.open = 0, []

    def copy(self, src, dst, ctx, fsdp=None, landing=None):
        return Copy(self, src, dst, ctx, self.fsdp if fsdp is None else fsdp, dst if landing is None else landing)

    def drain(self, copies=None):
        for copy in list(self.open) if copies is None else copies:
            copy.left()
            self.open.remove(copy)

    def finish(self):
        for copy in self.open:
            if not copy.arrived:
                copy.arrive()
        self.drain()


class Planner:
    def __init__(self):
        self.now, self.free, self.queue, self.serial = 0.0, {}, [], 0

    def ship(self, loads):
        end = self.now
        for link, us in loads.items():
            self.free[link] = max(self.now, self.free.get(link, 0.0)) + us
            end = max(end, self.free[link])
        return end + 1.5

    def later(self, when, run):
        self.serial += 1
        heapq.heappush(self.queue, (when, self.serial, run))

    def until(self, when):
        while self.queue and self.queue[0][0] <= max(self.now, when):
            at, _, run = heapq.heappop(self.queue)
            self.now = max(self.now, at)
            run()
            self.now += 0.2
        self.now = max(self.now, when)

    def compute(self, us, run, needs=0.0):
        self.until(needs)
        out = run()
        self.now += us
        return out

    def finish(self):
        self.until(1e9)


def road(axis, bit, us):
    if axis == "f":
        return {"y%d" % bit: us}
    return {1: {"core": us / 5}, 2: {"x": us}, 4: {"z": us}, 8: {"z": us, "mid": 2 * us}}.get(bit, {"far%d" % bit: us})


class Gather:
    def __init__(self, wire, c, f, nf, p, shard, full):
        rows = shard.shape[0]
        n = rows // p
        r = c % p
        self.a, self.b, self.z = [], [], []
        at = lambda owner, part: full.at[span(owner * rows + part * n, n)]
        sib = lambda i: flip(i, 1)
        for d in range(1, nf):
            fs = (f + nf - d) % nf
            self.a.append(wire.copy(shard.at[span(r * n, n)], at(f, r), c, (f + d) % nf, landing=at(fs, r)))
            near = []
            for j in range(1, p // 2):
                other, part = c, r
                for bit in (2, 4):
                    if (2 * j) & bit:
                        other, part = flip(other, bit), flip(part, bit)
                near.append((wire.copy(at(fs, r), at(fs, r), other, landing=at(fs, part)), part))
            self.b.append([copy for copy, _ in near])
            self.z.append([wire.copy(at(fs, q), at(fs, q), sib(c), landing=at(fs, sib(q))) for q in [r] + [q for _, q in near]])

    def begin(self):
        for copy in self.a:
            copy.start()

    def spread(self):
        for a, b, z in zip(self.a, self.b, self.z):
            a.arrive()
            for copy in b:
                copy.start()
            z[0].start()

    def pass_on(self):
        for b, z in zip(self.b, self.z):
            for near, sib in zip(b, z[1:]):
                near.arrive()
                sib.start()

    def finish(self):
        for z in self.z:
            for copy in z:
                copy.arrive()


def reduce_plan(rows, steps):
    plan = []
    for axis, bit in steps:
        halve = axis == "f" or rows % 32 == 0
        rows = rows // 2 if halve else rows
        plan.append((axis, bit, halve, rows))
    return plan


class Reduce:
    def __init__(self, wire, plan, c, f, nf, grad, boxes, steps, result, spread, lsem):
        self.wire, self.plan, self.c, self.f, self.grad, self.boxes, self.steps = wire, plan, c, f, grad, boxes, steps
        self.result, self.spread, self.lsem = result, spread, lsem
        self.base = f * (grad.shape[0] // nf)
        self.rows_us = 2 * 2 * grad.shape[1] / 98e3
        self.step, self.low, self.marks = 0, 0, []

    def peer(self, axis, bit):
        return (self.c, flip(self.f, bit)) if axis == "f" else (flip(self.c, bit), self.f)

    def send(self):
        if self.step == len(self.steps):
            return self.settle()
        axis, bit, halve, n = self.steps[self.step]
        mine = ((self.f if axis == "f" else self.c) // bit) % 2
        give = self.low + (1 - mine) * n if halve else self.low
        self.keep = self.low + mine * n if halve else self.low
        self.moving = self.wire.copy(self.grad.at[span(give, n)], self.boxes[self.step], *self.peer(axis, bit)).start()
        self.plan.later(self.plan.ship(road(axis, bit, n * self.rows_us)), self.add)

    def add(self):
        axis, bit, halve, n = self.steps[self.step]
        self.moving.arrive()
        box, grad, keep = self.boxes[self.step], self.grad, self.keep
        if not halve:
            self.wire.drain([self.moving])
        width = next(w for w in (128, 96, 64, 48, 32, 16) if n % w == 0)

        @pl.loop(0, n // width)
        def _(i):
            rows = span(keep + i * width, width)
            grad[rows, :] = (grad[rows, :].astype(F32) + box[span(i * width, width), :].astype(F32)).astype(BF)

        self.plan.now += n * grad.shape[1] / 4e5
        if axis == "c" and halve:
            self.marks.append((bit, keep, n))
        self.low, self.n = keep, n
        self.step += 1
        self.send()

    def settle(self):
        self.local = pltpu.make_async_copy(self.grad.at[span(self.low, self.n)], self.result(self.low - self.base, self.n), self.lsem)
        self.local.start()
        self.first = True
        self.give_back()

    def give_back(self):
        if self.local and (not self.first or not self.marks):
            self.local.wait()
            self.local = None
        if not self.marks:
            self.spread()
            return
        bit, low, n = self.marks.pop()
        mine = (self.c // bit) % 2
        there = low + n - 2 * n * mine
        src = self.grad.at[span(low, n)] if self.first else self.result(low - self.base, n)
        self.moving = self.wire.copy(src, self.result(low - self.base, n), flip(self.c, bit), landing=self.result(there - self.base, n)).start()
        self.first = False
        self.plan.later(self.plan.ship(road("c", bit, n * self.rows_us)), self.take_back)

    def take_back(self):
        self.moving.arrive()
        self.give_back()


def norm_rows(v):
    cen = v - jnp.mean(v, axis=-1, keepdims=True)
    rstd = lax.rsqrt(jnp.mean(cen * cen, axis=-1, keepdims=True) + EPS)
    return cen * rstd, rstd


def norm_back(grad, hat, rstd, gain):
    scaled = grad * gain
    return rstd * (scaled - jnp.mean(scaled, axis=-1, keepdims=True) - hat * jnp.mean(scaled * hat, axis=-1, keepdims=True))


def split3(v):
    hi = v.astype(BF).astype(F32)
    mid = (v - hi).astype(BF).astype(F32)
    return hi, mid, v - hi - mid


def layer(cfg, *refs):
    nc, nf, p, plans = cfg["nc"], cfg["nf"], cfg["p"], cfg["plans"]
    names = cfg["names"]
    R = dict(zip(names, refs, strict=True))
    x, cot, vec, lens = R["x"], R["cot"], R["vec"], R["lens"]
    wq_s, wo_s, wu_s, wd_s = R["wq_s"], R["wo_s"], R["wu_s"], R["wd_s"]
    wl, wo, wu, wd = R["wl"], R["wo"], R["wu"], R["wd"]
    vsum, bu = R["vsum"], R["bu"]
    xg, h1g, qp, kp, vp, of = R["xg"], R["h1g"], R["qp"], R["kp"], R["vp"], R["of"]
    omsg, oin, o2, res, h2, gb, gh = R["omsg"], R["oin"], R["o2"], R["res"], R["h2"], R["gb"], R["gh"]
    c, f = lax.axis_index("ctx"), lax.axis_index("fsdp")
    qs = nc // GROUPS
    g, m = c // qs, c % qs
    rows, D = x.shape
    T = rows // 2
    FF = wu.shape[1]
    core = c % 2
    sib = flip(c, 1)
    top = g // 4
    gq = g % 4
    odd = (gq % 2) == 1
    gf = flip(g, 4)
    far = flip(c, nc // 2)
    NQ = GROUPS * T
    NK = NQ * qs
    lsem = R["lsem"]
    wire = Wire(R["send"], R["recv"], f)

    done = set()

    def ready(i):
        if i not in done:
            loads[i].wait()
            done.add(i)

    lane = lax.broadcasted_iota(jnp.int32, (T, 128), 1)
    low = lane < HDIM

    off = (3 * (gq // 2) + gq % 2) * 128
    loads = []

    def load(src, dst):
        cp = pltpu.make_async_copy(src, dst, lsem.at[len(loads)])
        cp.start()
        loads.append(cp)

    nq = wq_s.shape[0]
    wcols = [span(i * D + off, 256, 128) for i in range(3)]
    for i in range(3):
        load(wq_s.at[:, wcols[i]], wl.at[span(f * nq, nq), i * 256 : (i + 1) * 256])
    for s, w in ((wo_s, wo), (wu_s, wu), (wd_s, wd)):
        load(s, w.at[span(f * s.shape[0], s.shape[0])])

    barrier = pltpu.get_barrier_semaphore()
    mates = [(((g + k) % GROUPS) * qs + m, f) for k in range(1, GROUPS)]
    mates += [(g * qs + (m + k) % qs, f) for k in range(1, qs)]
    mates += [(c, (f + k) % nf) for k in range(1, nf)]
    for mate in mates:
        pl.semaphore_signal(barrier, inc=1, device_id=mate, device_id_type=MESH)
    pl.semaphore_wait(barrier, len(mates))

    own_rows, other_rows = span(top * T, T), span((1 - top) * T, T)
    to_far = wire.copy(x.at[other_rows], xg.at[g], far, landing=xg.at[gf]).start()
    near = [(top * 4 + (gq + k) % 4, top * 4 + (gq + 4 - k) % 4) for k in (1, 2, 3)]
    own_out = [wire.copy(x.at[own_rows], xg.at[g], t * qs + m, landing=xg.at[s]).start() for t, s in near]
    far_out = [wire.copy(xg.at[gf], xg.at[gf], t * qs + m, landing=xg.at[flip(s, 4)]) for t, s in near]
    wq_out, vec_out = [], []
    for d in range(1, nf):
        fs = (f + nf - d) % nf
        vec_out.append(wire.copy(vec, R["vin"].at[d], c, (f + d) % nf).start())
        for i in range(3):
            cols = slice(i * 256, (i + 1) * 256)
            wq_out.append(wire.copy(wq_s.at[:, wcols[i]], wl.at[span(f * nq, nq), cols], c, (f + d) % nf,
                                    landing=wl.at[span(fs * nq, nq), cols]).start())
    weights = [Gather(wire, c, f, nf, p, s, w) for s, w in ((wo_s, wo), (wu_s, wu), (wd_s, wd))]
    for w in weights:
        w.begin()
    to_far.arrive()
    for copy in far_out:
        copy.start()
    xg[g] = x[own_rows, :]
    for copy in vec_out:
        copy.arrive()
    total = vec[...].astype(F32)
    for d in range(1, nf):
        total = total + R["vin"][d].astype(F32)
    vsum[...] = total
    for i in range(FF // D):
        bu[0:1, i * D : (i + 1) * D] = vsum[8 + i : 9 + i, :]
    for mb in range(2):
        pos = c * T + lax.broadcasted_iota(jnp.int32, (T, D), 0)
        live = pos < lens[mb]
        gb[mb * T : (mb + 1) * T, :] = jnp.where(live, cot[mb * T : (mb + 1) * T, :].astype(F32), 0.0).astype(BF)
    hd = D // 2
    mine, theirs = span(core * hd, hd, 128), span((1 - core) * hd, hd, 128)
    gh[0:rows, :] = gb[:, mine]
    lower, upper = slice(0, rows), slice(rows, 2 * rows)
    g_out = wire.copy(gb.at[:, theirs], gh.at[upper], sib).start()

    for i in range(3):
        ready(i)
    for copy in wq_out:
        copy.arrive()
    length = jnp.where(top == 0, lens[0], lens[1])
    kaug_hi = jnp.where((lane >= 64) & (lane < 68), 1.0, 0.0)
    kaug_lo = jnp.where(lane < 4, 1.0, 0.0)
    vaug_hi = jnp.where((lane >= 64) & (lane < 67), 1.0, 0.0)
    vaug_lo = jnp.where(lane < 3, 1.0, 0.0)
    one_hi, one_lo = jnp.where(lane == 64, 1.0, 0.0), jnp.where(lane == 0, 1.0, 0.0)
    bias_q = vsum[2:3, span(off, 256, 128)]
    bias_v = vsum[3:4, span(off, 256, 128)]

    def pick(t0, t1):
        return jnp.where(odd, t1, t0), jnp.where(odd, pltpu.roll(t0, HDIM, 1), t1)

    def project(s):
        hat, _ = norm_rows(xg[s].astype(F32))
        h1 = (hat * vsum[0:1, :] + vsum[1:2, :]).astype(BF)
        qrows = span(s * T, T, 128)
        krows = span((m * GROUPS + s) * T, T, 128)
        h1g[qrows, :] = h1
        y = dot_nn(h1, wl[...])
        q = y[:, 0:256] + bias_q
        v = y[:, 512:768] + bias_v
        qa, qc = pick(q[:, 0:128], q[:, 128:256])
        ka, kc = pick(y[:, 256:384], y[:, 384:512])
        va, vc = pick(v[:, 0:128], v[:, 128:256])
        pos = (s * qs + m) * T + lax.broadcasted_iota(jnp.int32, (T, 128), 0)
        bias = jnp.where(pos < length, 0.0, -1e30)
        k_hi = jnp.where(lane == 64, bias, kaug_hi)
        k_lo = jnp.where(lane == 0, bias, kaug_lo)
        qa, qc = qa.astype(BF).astype(F32) * 0.125, qc.astype(BF).astype(F32) * 0.125
        qp[0, qrows, :] = jnp.where(low, qa, one_hi).astype(BF)
        qp[1, qrows, :] = jnp.where(low, one_lo, qa).astype(BF)
        qp[2, qrows, :] = jnp.where(low, qc, one_hi).astype(BF)
        kp[0, krows, :] = jnp.where(low, ka, k_hi).astype(BF)
        kp[1, krows, :] = jnp.where(low, k_lo, ka).astype(BF)
        kp[2, krows, :] = jnp.where(low, kc, k_hi).astype(BF)
        vp[0, krows, :] = jnp.where(low, va, vaug_hi).astype(BF)
        vp[1, krows, :] = jnp.where(low, vaug_lo, va).astype(BF)
        vp[2, krows, :] = jnp.where(low, vc, vaug_hi).astype(BF)

    def share(first):
        out = []
        for j in range(1, qs):
            for ref in (kp, vp):
                at = lambda who: ref.at[:, span((who * GROUPS + first) * T, 4 * T, 128), :]
                out.append(wire.copy(at(m), at(m), g * qs + (m + j) % qs, landing=at((m + qs - j) % qs)).start())
        return out

    for copy in own_out:
        copy.arrive()
    pl.loop(0, 4)(lambda i: project(top * 4 + i))
    shares = share(top * 4)
    for copy in far_out:
        copy.arrive()
    pl.loop(0, 4)(lambda i: project((1 - top) * 4 + i))
    shares += share((1 - top) * 4)
    weights[0].spread()
    weights[1].spread()
    for copy in shares:
        copy.arrive()
    weights[2].spread()

    tq = cfg["tq"]
    lane_q = lax.broadcasted_iota(jnp.int32, (tq, 128), 1)

    def attend(h):
        base = 0 if h == 1 else HDIM

        @pl.loop(0, NQ // tq)
        def _(i):
            at = span(i * tq, tq, 128)
            q = qp[h, at, :]
            s = dot_nt(q, kp[h])
            peak = jnp.max(s, axis=1, keepdims=True)
            e = jnp.exp(s - peak).astype(BF)
            o = dot_nn(e, vp[h])
            l = o[:, base : base + 1]
            of[h, at, :] = o / l
            a, b, d = split3(-(peak + jnp.log(l)))
            q = q.astype(F32)
            q = jnp.where(lane_q == base + 1, a, jnp.where(lane_q == base + 2, b, jnp.where(lane_q == base + 3, d, q)))
            qp[h, at, :] = q.astype(BF)

    def deal(msg, box, half):
        box[half, g] = msg[half, g]
        out = []
        for k in range(1, GROUPS):
            t, s = (g + k) % GROUPS, (g + GROUPS - k) % GROUPS
            out.append(wire.copy(msg.at[half, t], box.at[half, g], t * qs + m, landing=box.at[half, s]).start())
        return out

    attend(0)
    attend(1)

    @pl.loop(0, GROUPS)
    def _(s):
        at = span(s * T, T, 128)
        omsg[0, s] = jnp.where(low, of[0, at, :], of[1, at, :]).astype(BF)

    o_out = deal(omsg, oin, 0)
    weights[0].pass_on()
    attend(2)

    @pl.loop(0, GROUPS)
    def _(s):
        omsg[1, s] = of[2, span(s * T, T, 128), :].astype(BF)

    o_out += deal(omsg, oin, 1)
    weights[1].pass_on()
    weights[2].pass_on()
    for copy in o_out:
        copy.arrive()

    def tiles(jp):
        return [slice((3 * jp + i) * 128, (3 * jp + i + 1) * 128) for i in range(3)]

    for mb in range(2):
        for jp in range(2):
            g0 = 4 * mb + 2 * jp
            at = slice(mb * T, (mb + 1) * T)
            t0, t1, t2 = tiles(jp)
            o2[at, t0] = oin[0, g0]
            o2[at, t1] = jnp.where(low, oin[1, g0].astype(F32), pltpu.roll(oin[1, g0 + 1].astype(F32), HDIM, 1)).astype(BF)
            o2[at, t2] = oin[0, g0 + 1]
    o_pair = wire.copy(o2.at[lower], o2.at[upper], sib).start()
    ready(3)
    weights[0].finish()
    res[...] = x[...].astype(F32) + dot_nn(o2[lower, :], wo[...]) + vsum[4:5, :]
    hat2, _ = norm_rows(res[...])
    h2[lower, :] = (hat2 * vsum[5:6, :] + vsum[6:7, :]).astype(BF)
    h_pair = wire.copy(h2.at[lower], h2.at[upper], sib).start()
    for i in (1, 2):
        ready(3 + i)
        weights[i].finish()

    a2, duh, dus, dbu, acc, dh2 = R["a2"], R["duh"], R["dus"], R["dbu"], R["acc"], R["dh2"]
    acc[...] = jnp.zeros_like(acc)
    dh2[...] = jnp.zeros_like(dh2)
    hf = FF // 2

    def hidden(which, keep):
        @pl.loop(0, hf // WIDE)
        def _(i):
            col = which * hf + i * WIDE
            cols = span(col, WIDE, 128)
            u = dot_nn(h2[lower, :], wu[:, cols]) + bu[:, cols]
            phi = 0.5 + 0.5 * lax.erf(u * 0.7071067811865476)
            a = (u * phi).astype(BF)
            a2[lower, cols] = a
            da = dot_nt(gb[...], wd[span(col, WIDE, 128), :])
            slope = phi + u * (0.3989422804014327 * jnp.exp(-0.5 * u * u))
            du = (da * slope).astype(BF)
            keep[0:rows, span(i * WIDE, WIDE, 128)] = du
            dbu[:, cols] = jnp.sum(du.astype(F32), axis=0, keepdims=True)
            acc[...] += dot_nn(a, wd[span(col, WIDE, 128), :])
            dh2[...] += dot_nt(du, wu[:, cols])

    hidden(1 - core, dus)
    du_pair = wire.copy(dus, duh.at[upper], sib).start()
    half_cols = lambda which: span(which * hf, hf, 128)
    a_pair = [wire.copy(a2.at[lower, half_cols(1 - core)], a2.at[upper, half_cols(1 - core)], sib, landing=a2.at[upper, half_cols(core)]).start()]
    hidden(core, duh)
    a_pair.append(wire.copy(a2.at[lower, half_cols(core)], a2.at[upper, half_cols(core)], sib, landing=a2.at[upper, half_cols(1 - core)]).start())
    R["out"][...] = (res[...] + acc[...] + vsum[7:8, :]).astype(BF)
    plan = Planner()
    a_here = plan.ship({"core": 5.0})
    dr, dbh, dbs, dmsg, doin = R["dr"], R["dbh"], R["dbs"], omsg, R["doin"]
    dvb = R["dvb"]
    gd, gu, go, gqr = wd.at[:, 0:hd], wu.at[:, 0:hf], wo.at[:, 0:hd], wu.at[:, hf : hf + D]

    def residual_back():
        hat2, rstd2 = norm_rows(res[...])
        dvb[0, 5:6, :] = jnp.sum(dh2[...] * hat2, axis=0, keepdims=True)
        dvb[0, 6:7, :] = jnp.sum(dh2[...], axis=0, keepdims=True)
        dr[...] = gb[...].astype(F32) + norm_back(dh2[...], hat2, rstd2, vsum[5:6, :])
        db = dr[...].astype(BF)
        dbs[...] = db
        dvb[0, 4:5, :] = jnp.sum(db.astype(F32), axis=0, keepdims=True)
        dvb[0, 7:8, :] = jnp.sum(gb[...].astype(F32), axis=0, keepdims=True)
        dbh[0:rows, :] = dbs[:, mine]
        db_pair = wire.copy(dbs.at[:, theirs], dbh.at[upper], sib).start()
        acc[...] = dot_nt(db, wo[...])
        wire.drain(o_out)
        for t in range(GROUPS):
            mb, jj = t // 4, t % 4
            at = slice(mb * T, (mb + 1) * T)
            t0, t1, t2 = tiles(jj // 2)
            dmsg[0, t] = acc[at, t2 if jj % 2 else t0].astype(BF)
            single = acc[at, t1]
            dmsg[1, t] = (pltpu.roll(single, HDIM, 1) if jj % 2 else single).astype(BF)
        do_out = [deal(dmsg, doin, 0), deal(dmsg, doin, 1)]
        load = {"x": 2.7, "z": 4.0, "mid": 5.4}
        here = [plan.ship(load), plan.ship(load)]
        for w in weights:
            for copies in [w.a] + w.b + w.z:
                wire.drain(copies)
        wire.drain(far_out)
        return db_pair, do_out, here

    db_pair, do_out, do_here = plan.compute(2.0, residual_back)

    def shard(ref, half, c0, c1, lead=()):
        return lambda lo, n: ref.at[lead + (span(lo, n), span(core * half + c0, c1 - c0, 128))]

    lone = []

    def sibling(ref, half, c0, c1):
        def go():
            at = lambda which: ref.at[:, span(which * half + c0, c1 - c0, 128)]
            copy = wire.copy(at(core), at(core), sib, landing=at(1 - core)).start()
            plan.later(plan.ship({"core": 1.0}), copy.arrive)
        return go

    def reduction(k, j, grad, ref, half, c0, c1):
        boxes = [R[f"box_{k}{j}{i}"] for i in range(len(plans[k]))]
        Reduce(wire, plan, c, f, nf, grad.at[:, c0:c1], boxes, plans[k], shard(ref, half, c0, c1), sibling(ref, half, c0, c1),
               lsem.at[7 + len(lone)]).send()
        lone.append(k)

    def down_grads():
        for copy in a_pair:
            copy.arrive()
        g_out.arrive()

        @pl.loop(0, FF // WIDE)
        def _(i):
            at = span(i * WIDE, WIDE, 128)
            wd[at, 0:hd] = dot_tn(a2[:, at], gh[...]).astype(BF)

        for j, (c0, c1) in enumerate(cfg["cuts"]["d"]):
            reduction("d", j, gd, R["fd"], hd, c0, c1)

    plan.compute(2.0, down_grads, a_here)

    def up_grads():
        h_pair.arrive()
        du_pair.arrive()
        for j, (c0, c1) in enumerate(cfg["cuts"]["u"]):
            wu[:, c0:c1] = dot_tn(h2[...], duh[:, c0:c1]).astype(BF)
            reduction("u", j, gu, R["fu"], hf, c0, c1)

    plan.compute(2.2, up_grads)

    def out_grads():
        o_pair.arrive()
        db_pair.arrive()
        wo[:, 0:hd] = dot_tn(o2[...], dbh[...]).astype(BF)
        for j, (c0, c1) in enumerate(cfg["cuts"]["o"]):
            reduction("o", j, go, R["fo"], hd, c0, c1)

    plan.compute(0.7, out_grads)

    dop, dka, dva, dkv, dkvin, dqkv = (R[k] for k in ("dop", "dka", "dva", "dkv", "dkvin", "dqkv"))
    dqa = of
    tb, kc = cfg["tb"], cfg["kc"]
    lane_b = lax.broadcasted_iota(jnp.int32, (tb, 128), 1)

    def prepare(h):
        half = 1 if h == 2 else 0
        base = 0 if h == 1 else HDIM

        @pl.loop(0, GROUPS)
        def _(s):
            at = span(s * T, T, 128)
            d = doin[half, s].astype(F32)
            d = jnp.where(low, 0.0, d) if h == 1 else jnp.where(low, d, 0.0)
            a, b, e = split3(-jnp.sum(d * of[h, at, :], axis=1, keepdims=True))
            d = jnp.where(lane == base, a, jnp.where(lane == base + 1, b, jnp.where(lane == base + 2, e, d)))
            dop[h, at, :] = d.astype(BF)

    def retrace(h, first, last):
        keep = (lambda v: jnp.where(lane_b < HDIM, 0.0, v)) if h == 1 else (lambda v: jnp.where(lane_b < HDIM, v, 0.0))
        if h != 1 and first == 0:
            dka[...] = jnp.zeros((NK, 128), F32)
            dva[...] = jnp.zeros((NK, 128), F32)

        @pl.loop(first, last)
        def _(i):
            at = span(i * tb, tb, 128)
            q, d = qp[h, at, :], dop[h, at, :]
            q0, d0 = keep(q.astype(F32)).astype(BF), keep(d.astype(F32)).astype(BF)
            dq = jnp.zeros((tb, 128), F32)
            for j in range(NK // kc):
                ks = slice(j * kc, (j + 1) * kc)
                k, v = kp[h, ks, :], vp[h, ks, :]
                pt = jnp.exp(dot_nt(k, q))
                ds = (pt * dot_nt(v, d)).astype(BF)
                dva[ks, :] += dot_nn(pt.astype(BF), d0)
                dka[ks, :] += dot_nn(ds, q0)
                dq = dq + dot_tn(ds, k)
            dqa[h, at, :] = dq * 0.125

    def trade(half):
        out = []
        for j in range(1, qs):
            part = (m + j) % qs

            @pl.loop(0, GROUPS)
            def _(s):
                at = span((part * GROUPS + s) * T, T, 128)
                to = span(s * T, T, 128)
                dkv[j - 1, 0, to, :] = dka[at, :].astype(BF)
                dkv[j - 1, 1, to, :] = dva[at, :].astype(BF)

            out.append(wire.copy(dkv.at[j - 1], dkvin.at[j - 1, half], g * qs + part).start())
        return out

    def place(half, base, at, tile):
        if half == 0:
            dqkv[at, base : base + 128] = jnp.where(odd, dqkv[at, base : base + 128].astype(F32), tile).astype(BF)
            dqkv[at, base + 128 : base + 256] = jnp.where(odd, tile, dqkv[at, base + 128 : base + 256].astype(F32)).astype(BF)
        else:
            turned = pltpu.roll(tile, HDIM, 1)
            dqkv[at, base : base + 128] = jnp.where(odd, turned, dqkv[at, base : base + 128].astype(F32)).astype(BF)
            dqkv[at, base + 128 : base + 256] = jnp.where(odd, dqkv[at, base + 128 : base + 256].astype(F32), tile).astype(BF)

    def settle_heads(half, trades):
        for copy in trades:
            copy.arrive()
        wire.drain(trades)
        pair = half == 0

        @pl.loop(0, GROUPS)
        def _(s):
            at = span(s * T, T, 128)
            mine_at = span((m * GROUPS + s) * T, T, 128)
            if pair:
                tile = jnp.where(low, dqa[0, at, :], dqa[1, at, :])
            else:
                tile = jnp.where(low, dqa[2, at, :], 0.0)
            place(half, 0, at, tile)
            for which, acc_ref in ((0, dka), (1, dva)):
                tile = acc_ref[mine_at, :]
                for j in range(1, qs):
                    tile = tile + dkvin[j - 1, half, which, at, :].astype(F32)
                place(half, 256 * (which + 1), at, tile)

    def retrace_all(h):
        n = NQ // tb
        for first, last in ((0, n // 2), (n // 2, n)):
            plan.compute(3.2, lambda: retrace(h, first, last))

    def ready_pair():
        dqkv[...] = jnp.zeros_like(dqkv)
        for copy in do_out[0]:
            copy.arrive()
        prepare(0)
        prepare(1)

    def ready_single():
        for copy in do_out[1]:
            copy.arrive()
        prepare(2)

    plan.compute(1.9, ready_pair, do_here[0])
    retrace_all(0)
    retrace_all(1)
    trades = plan.compute(0.5, lambda: trade(0))
    pair_here = plan.ship({"core": 3.0})
    plan.compute(1.0, ready_single, do_here[1])
    plan.compute(1.0, lambda: settle_heads(0, trades), pair_here)
    retrace_all(2)
    trades = plan.compute(0.5, lambda: trade(1))
    plan.compute(1.0, lambda: settle_heads(1, trades), plan.ship({"core": 3.0}))

    dh1p, dh1in, dh1, farbox = xg, R["dh1in"], dh2, R["farbox"]
    gqh, box_c = wu.at[:, hf + D : hf + D + hd], R["box_c"]

    def inputs_back():
        pl.loop(0, GROUPS)(lambda s: dh1p.__setitem__(s, dot_nt(dqkv[span(s * T, T, 128), :], wl[...]).astype(BF)))
        out = [wire.copy(dh1p.at[flip(t, 4)], dh1in.at[k, 1], t * qs + m).start() for k, (t, s) in enumerate(near)]
        out += [wire.copy(dh1p.at[t], dh1in.at[k, 0], t * qs + m).start() for k, (t, s) in enumerate(near)]
        return out

    dh_out = plan.compute(2.0, inputs_back)
    dh_here = [plan.ship({"x": 8.0, "z": 8.0}), plan.ship({"x": 8.0, "z": 8.0})]

    def qkv_grads():
        for i in range(0, D, 256):
            gqr[:, i : i + 256] = dot_tn(h1g[...], dqkv[:, i : i + 256]).astype(BF)
        return wire.copy(gqr.at[:, theirs], box_c, sib).start()

    gq_pair = plan.compute(2.0, qkv_grads)
    gq_here = plan.ship({"core": 2.0})

    def column_sums():
        colsum = lax.fori_loop(
            0, GROUPS, lambda i, t: t + jnp.sum(dqkv[span(i * T, T, 128), :].astype(F32), axis=0, keepdims=True), jnp.zeros((1, D), F32)
        )
        dvb[0, 2:4, :] = jnp.zeros((2, D), F32)
        dvb[0, 12:16, :] = jnp.zeros((4, D), F32)
        dvb[0, 2:3, span(off, 256, 128)] = colsum[:, 0:256]
        dvb[0, 3:4, span(off, 256, 128)] = colsum[:, 512:768]
        for i in range(FF // D):
            dvb[0, 8 + i : 9 + i, :] = dbu[0:1, i * D : (i + 1) * D]

    plan.compute(0.5, column_sums)
    fq = R["fq"]

    def spread_q():
        moves = [(2, [gq]), (1, [gq, flip(gq, 2)]), (0, None)]

        def go():
            bit, have = moves.pop(0)
            if bit:
                ref = lambda jj: fq.at[jj, :, span(core * hd, hd, 128)]
                mate = flip(c, bit * qs)
                copies = [wire.copy(ref(j), ref(j), mate, landing=ref(flip(j, bit))).start() for j in have]
                us = len(have) * fq.shape[1] * hd * 4 / 98e3
            else:
                at = lambda which: fq.at[:, :, span(which * hd, hd, 128)]
                copies = [wire.copy(at(core), at(core), sib, landing=at(1 - core)).start()]
                us = 12.0

            def come():
                for copy in copies:
                    copy.arrive()
                if moves:
                    go()

            plan.later(plan.ship(road("c", 2 * bit if bit else 1, us)), come)

        go()

    def sum_q():
        gq_pair.arrive()
        gqh[...] = (gqr[:, mine].astype(F32) + box_c[...].astype(F32)).astype(BF)
        Reduce(wire, plan, c, f, nf, gqh, [R[f"box_q0{i}"] for i in range(len(plans["q"]))], plans["q"],
               shard(fq, hd, 0, hd, (gq,)), spread_q, lsem.at[6]).send()

    plan.compute(0.5, sum_q, gq_here)

    def total_of(which, block):
        s = dh1p[block].astype(F32)
        for k in range(3):
            s = s + dh1in[k, which].astype(F32)
        return s

    def far_total():
        for copy in dh_out[:3]:
            copy.arrive()
        farbox[0] = total_of(1, gf).astype(BF)
        return wire.copy(farbox.at[0], farbox.at[1], far).start()

    far_back = plan.compute(0.5, far_total, dh_here[0])
    far_here = plan.ship({"z": 4.0, "mid": 8.0})

    def near_total():
        for copy in dh_out[3:]:
            copy.arrive()
        dh1[own_rows, :] = total_of(0, g)

    plan.compute(0.5, near_total, dh_here[1])
    dvin = R["dvin"]
    bits = [("c", 1 << b) for b in range(nc.bit_length() - 1)] + [("f", 1 << b) for b in range(nf.bit_length() - 1)]

    def vectors(i=0):
        if i == len(bits):
            R["dvec"][...] = dvb[i]
            return
        axis, bit = bits[i]
        peer = (c, flip(f, bit)) if axis == "f" else (flip(c, bit), f)
        moved = wire.copy(dvb.at[i], dvin.at[i], *peer).start()

        def come():
            moved.arrive()
            dvb[i + 1] = dvb[i] + dvin[i]
            vectors(i + 1)

        plan.later(plan.ship(road(axis, bit, 1.0)), come)

    def finish_inputs():
        far_back.arrive()
        dh1[other_rows, :] = farbox[1].astype(F32)
        hat1, rstd1 = norm_rows(x[...].astype(F32))
        dvb[0, 0:1, :] = jnp.sum(dh1[...] * hat1, axis=0, keepdims=True)
        dvb[0, 1:2, :] = jnp.sum(dh1[...], axis=0, keepdims=True)
        vectors()
        R["gin"][...] = (dr[...] + norm_back(dh1[...], hat1, rstd1, vsum[0:1, :])).astype(BF)

    plan.compute(1.7, finish_inputs, far_here)
    plan.finish()
    wire.drain()


def call(nc, nf, x, cot, vec, lens, wq, wo, wu, wd):
    qs = nc // GROUPS
    R, D = x.shape
    T, FF = R // 2, wu.shape[1]
    NQ, NK = GROUPS * T, GROUPS * T * qs
    hd, hf = D // 2, FF // 2
    p = next(p for p in (8, 4, 2) if nc % p == 0 and all(w.shape[0] % (16 * p) == 0 for w in (wo, wu, wd)))
    fbits = [("f", 1 << b) for b in reversed(range(nf.bit_length() - 1))]
    cbits = [("c", 1 << b) for b in range(1, nc.bit_length() - 1)]
    qbits = [("c", 1 << b) for b in range(1, qs.bit_length() - 1)] + [("c", nc // 2)]
    plans = {"d": reduce_plan(FF, fbits + cbits), "u": reduce_plan(D, fbits + cbits), "o": reduce_plan(D, fbits + cbits),
             "q": reduce_plan(D, fbits + qbits)}
    sds, dma = jax.ShapeDtypeStruct, pltpu.SemaphoreType.DMA
    any_, vm, sm = (pl.BlockSpec(memory_space=s) for s in (pl.ANY, pltpu.VMEM, pltpu.SMEM))
    ins = ["x", "cot", "vec", "lens", "wq_s", "wo_s", "wu_s", "wd_s"]
    outs = {"out": sds((R, D), BF), "gin": sds((R, D), BF), "dvec": sds((16, D), F32), "fq": sds((4, D // nf, D), BF),
            "fo": sds((D // nf, D), BF), "fu": sds((D // nf, FF), BF), "fd": sds((FF // nf, D), BF)}
    nb = nc.bit_length() + nf.bit_length() - 2
    b, s = (lambda *shape: pltpu.VMEM(shape, BF)), (lambda *shape: pltpu.VMEM(shape, F32))
    scratch = {
        "wl": b(D, D), "wo": b(D, D), "wu": b(D, FF), "wd": b(FF, D), "vsum": s(16, D), "bu": s(1, FF), "vin": b(nf, 16, D),
        "xg": b(GROUPS, T, D), "h1g": b(NQ, D), "qp": b(3, NQ, 128), "kp": b(3, NK, 128), "vp": b(3, NK, 128), "of": s(3, NQ, 128),
        "omsg": b(2, GROUPS, T, 128), "oin": b(2, GROUPS, T, 128), "o2": b(2 * R, D), "res": s(R, D), "h2": b(2 * R, D), "gb": b(R, D),
        "gh": b(2 * R, hd), "a2": b(2 * R, FF), "duh": b(2 * R, hf), "dus": b(R, hf), "dbu": s(1, FF), "acc": s(R, D), "dh2": s(R, D),
        "dr": s(R, D), "dbh": b(2 * R, hd), "dbs": b(R, D), "doin": b(2, GROUPS, T, 128),
        "dop": b(3, NQ, 128), "dka": s(NK, 128), "dva": s(NK, 128),
        "dkv": b(qs - 1, 2, NQ, 128), "dkvin": b(qs - 1, 2, 2, NQ, 128), "dqkv": b(NQ, D),
        "dh1in": b(3, 2, T, D), "farbox": b(2, T, D),
        "box_c": b(D, hd), "dvb": s(nb + 1, 16, D), "dvin": s(nb, 16, D),
        "lsem": dma((16,)), "send": dma((400,)), "recv": dma((400,)),
    }
    cuts = {"d": [(i, i + 128) for i in range(0, hd, 128)], "u": [(i, i + 512) for i in range(0, hf, 512)], "o": [(0, hd)], "q": [(0, hd)]}
    for k in cuts:
        for j, (c0, c1) in enumerate(cuts[k]):
            for i, (_, _, _, n) in enumerate(plans[k]):
                scratch[f"box_{k}{j}{i}"] = b(n, c1 - c0)
    cfg = dict(nc=nc, nf=nf, p=p, plans=plans, names=ins + list(outs) + list(scratch), cuts=cuts, tq=128, tb=256, kc=512)
    return pl.pallas_call(
        functools.partial(layer, cfg),
        out_shape=list(outs.values()),
        in_specs=[vm, vm, vm, sm, any_, any_, any_, any_],
        out_specs=[vm, vm, vm, any_, any_, any_, any_],
        scratch_shapes=list(scratch.values()),
        compiler_params=pltpu.CompilerParams(collective_id=0, has_side_effects=True, vmem_limit_bytes=62_464 * 1024),
    )(x, cot, vec, lens, wq, wo, wu, wd)


def body(inputs, cotangent, lengths, g1, b1, w_qkv, bias_q, bias_v, w_out, bias_out, g2, b2, w_up, bias_up, w_down, bias_down, nc, nf):
    MB, _, T, D = inputs.shape
    f = lax.axis_index("fsdp")
    small = [g1, b1, bias_q, bias_v, bias_out, g2, b2, bias_down, bias_up]
    flat = jnp.concatenate([jnp.tile(v, nf) for v in small])
    owner = jnp.concatenate([jnp.repeat(jnp.arange(nf), v.shape[0]) for v in small])
    vec = jnp.where(owner == f, flat, 0).astype(BF).reshape(-1, D)
    vec = jnp.pad(vec, ((0, 16 - vec.shape[0]), (0, 0)))
    out, gin, dvec, fq, fo, fu, fd = call(nc, nf, inputs.reshape(MB * T, D), cotangent.reshape(MB * T, D), vec, lengths[:, 0],
                                          w_qkv, w_out, w_up, w_down)
    n = g1.shape[0]
    row = lambda i: lax.dynamic_slice(dvec[i], (f * n,), (n,))
    up = lax.dynamic_slice(dvec[8:12].reshape(-1), (f * bias_up.shape[0],), bias_up.shape)
    parts = fq.astype(F32)
    cols = []
    for t in range(3):
        for a in range(2):
            x0, x1 = parts[2 * a, :, 256 * t : 256 * t + 256], parts[2 * a + 1, :, 256 * t : 256 * t + 256]
            cols += [x0[:, :128], x0[:, 128:] + x1[:, :128], x1[:, 128:]]
    shape = (MB, 1, T, D)
    return (out.reshape(shape), gin.reshape(shape), row(0), row(1), jnp.concatenate(cols, axis=1), row(2), row(3), fo.astype(F32), row(4),
            row(5), row(6), fu.astype(F32), up, fd.astype(F32), row(7))


def solution(mesh):
    nc, nf = mesh.shape["ctx"], mesh.shape["fsdp"]
    act = P(None, "fsdp", "ctx", None)
    one, two = P("fsdp"), P("fsdp", None)
    return jax.shard_map(
        functools.partial(body, nc=nc, nf=nf),
        mesh=mesh,
        in_specs=(act, act, P(None, "fsdp"), one, one, two, one, one, two, one, one, one, two, one, two, one),
        out_specs=(act, act, one, one, two, one, one, two, one, one, one, two, one, two, one),
        check_vma=False,
    )
```

```python
import functools
import heapq

import jax
import jax.numpy as jnp
from jax import lax
from jax.experimental import pallas as pl
from jax.experimental.pallas import tpu as pltpu
from jax.sharding import PartitionSpec as P

HEADS = 12
HDIM = 64
GROUPS = 8
EPS = 1e-6
BF = jnp.bfloat16
F32 = jnp.float32
WIDE = 512
MESH = pl.DeviceIdType.MESH


def dot_nn(a, b):
    return lax.dot_general(a, b, (((1,), (0,)), ((), ())), preferred_element_type=F32)


def dot_nt(a, b):
    return lax.dot_general(a, b, (((1,), (1,)), ((), ())), preferred_element_type=F32)


def dot_tn(a, b):
    return lax.dot_general(a, b, (((0,), (0,)), ((), ())), preferred_element_type=F32)


def flip(index, bit):
    return index + bit - 2 * bit * ((index // bit) % 2)


def span(start, size, unit=16):
    return pl.ds(pl.multiple_of(start, unit), size)


class Copy:
    def __init__(self, wire, src, dst, ctx, fsdp, landing):
        self.wire, self.src, self.dst, self.landing = wire, src, dst, landing
        self.ctx, self.fsdp, self.i = ctx, fsdp, wire.count
        self.arrived = False
        wire.count += 1

    def of(self, dst):
        return pltpu.make_async_remote_copy(
            src_ref=self.src, dst_ref=dst, send_sem=self.wire.send.at[self.i], recv_sem=self.wire.recv.at[self.i],
            device_id=(self.ctx, self.fsdp), device_id_type=MESH,
        )

    def start(self):
        self.of(self.dst).start()
        self.wire.open.append(self)
        return self

    def arrive(self):
        self.of(self.landing).wait_recv()
        self.arrived = True

    def left(self):
        self.of(self.dst).wait_send()


class Wire:
    def __init__(self, send, recv, fsdp):
        self.send, self.recv, self.fsdp = send, recv, fsdp
        self.count, self.open = 0, []

    def copy(self, src, dst, ctx, fsdp=None, landing=None):
        return Copy(self, src, dst, ctx, self.fsdp if fsdp is None else fsdp, dst if landing is None else landing)

    def drain(self, copies=None):
        for copy in list(self.open) if copies is None else copies:
            copy.left()
            self.open.remove(copy)

    def finish(self):
        for copy in self.open:
            if not copy.arrived:
                copy.arrive()
        self.drain()


class Planner:
    def __init__(self):
        self.now, self.free, self.queue, self.serial = 0.0, {}, [], 0

    def ship(self, loads):
        end = self.now
        for link, us in loads.items():
            self.free[link] = max(self.now, self.free.get(link, 0.0)) + us
            end = max(end, self.free[link])
        return end + 1.5

    def later(self, when, run):
        self.serial += 1
        heapq.heappush(self.queue, (when, self.serial, run))

    def until(self, when):
        while self.queue and self.queue[0][0] <= max(self.now, when):
            at, _, run = heapq.heappop(self.queue)
            self.now = max(self.now, at)
            run()
            self.now += 0.2
        self.now = max(self.now, when)

    def compute(self, us, run, needs=0.0):
        self.until(needs)
        out = run()
        self.now += us
        return out

    def finish(self):
        self.until(1e9)


def road(axis, bit, us):
    if axis == "f":
        return {"y%d" % bit: us}
    return {1: {"core": us / 5}, 2: {"x": us}, 4: {"z": us}, 8: {"z": us, "mid": 2 * us}}.get(bit, {"far%d" % bit: us})


class Gather:
    def __init__(self, wire, c, f, nf, p, shard, full):
        rows = shard.shape[0]
        n = rows // p
        r = c % p
        self.a, self.b, self.z = [], [], []
        at = lambda owner, part: full.at[span(owner * rows + part * n, n)]
        sib = lambda i: flip(i, 1)
        for d in range(1, nf):
            fs = (f + nf - d) % nf
            self.a.append(wire.copy(shard.at[span(r * n, n)], at(f, r), c, (f + d) % nf, landing=at(fs, r)))
            near = []
            for j in range(1, p // 2):
                other, part = c, r
                for bit in (2, 4):
                    if (2 * j) & bit:
                        other, part = flip(other, bit), flip(part, bit)
                near.append((wire.copy(at(fs, r), at(fs, r), other, landing=at(fs, part)), part))
            self.b.append([copy for copy, _ in near])
            self.z.append([wire.copy(at(fs, q), at(fs, q), sib(c), landing=at(fs, sib(q))) for q in [r] + [q for _, q in near]])

    def begin(self):
        for copy in self.a:
            copy.start()

    def spread(self):
        for a, b, z in zip(self.a, self.b, self.z):
            a.arrive()
            for copy in b:
                copy.start()
            z[0].start()

    def pass_on(self):
        for b, z in zip(self.b, self.z):
            for near, sib in zip(b, z[1:]):
                near.arrive()
                sib.start()

    def finish(self):
        for z in self.z:
            for copy in z:
                copy.arrive()


def reduce_plan(rows, steps):
    plan = []
    for axis, bit in steps:
        halve = axis == "f" or rows % 32 == 0
        rows = rows // 2 if halve else rows
        plan.append((axis, bit, halve, rows))
    return plan


class Reduce:
    def __init__(self, wire, plan, c, f, nf, grad, boxes, steps, result, spread, lsem):
        self.wire, self.plan, self.c, self.f, self.grad, self.boxes, self.steps = wire, plan, c, f, grad, boxes, steps
        self.result, self.spread, self.lsem = result, spread, lsem
        self.base = f * (grad.shape[0] // nf)
        self.rows_us = 2 * 2 * grad.shape[1] / 98e3
        self.step, self.low, self.marks = 0, 0, []

    def peer(self, axis, bit):
        return (self.c, flip(self.f, bit)) if axis == "f" else (flip(self.c, bit), self.f)

    def send(self):
        if self.step == len(self.steps):
            return self.settle()
        axis, bit, halve, n = self.steps[self.step]
        mine = ((self.f if axis == "f" else self.c) // bit) % 2
        give = self.low + (1 - mine) * n if halve else self.low
        self.keep = self.low + mine * n if halve else self.low
        self.moving = self.wire.copy(self.grad.at[span(give, n)], self.boxes[self.step], *self.peer(axis, bit)).start()
        self.plan.later(self.plan.ship(road(axis, bit, n * self.rows_us)), self.add)

    def add(self):
        axis, bit, halve, n = self.steps[self.step]
        self.moving.arrive()
        box, grad, keep = self.boxes[self.step], self.grad, self.keep
        if not halve:
            self.wire.drain([self.moving])
        width = next(w for w in (128, 96, 64, 48, 32, 16) if n % w == 0)

        @pl.loop(0, n // width)
        def _(i):
            rows = span(keep + i * width, width)
            grad[rows, :] = (grad[rows, :].astype(F32) + box[span(i * width, width), :].astype(F32)).astype(BF)

        self.plan.now += n * grad.shape[1] / 4e5
        if axis == "c" and halve:
            self.marks.append((bit, keep, n))
        self.low, self.n = keep, n
        self.step += 1
        self.send()

    def settle(self):
        self.local = pltpu.make_async_copy(self.grad.at[span(self.low, self.n)], self.result(self.low - self.base, self.n), self.lsem)
        self.local.start()
        self.first = True
        self.give_back()

    def give_back(self):
        if self.local and (not self.first or not self.marks):
            self.local.wait()
            self.local = None
        if not self.marks:
            self.spread()
            return
        bit, low, n = self.marks.pop()
        mine = (self.c // bit) % 2
        there = low + n - 2 * n * mine
        src = self.grad.at[span(low, n)] if self.first else self.result(low - self.base, n)
        self.moving = self.wire.copy(src, self.result(low - self.base, n), flip(self.c, bit), landing=self.result(there - self.base, n)).start()
        self.first = False
        self.plan.later(self.plan.ship(road("c", bit, n * self.rows_us)), self.take_back)

    def take_back(self):
        self.moving.arrive()
        self.give_back()


def norm_rows(v):
    cen = v - jnp.mean(v, axis=-1, keepdims=True)
    rstd = lax.rsqrt(jnp.mean(cen * cen, axis=-1, keepdims=True) + EPS)
    return cen * rstd, rstd


def norm_back(grad, hat, rstd, gain):
    scaled = grad * gain
    return rstd * (scaled - jnp.mean(scaled, axis=-1, keepdims=True) - hat * jnp.mean(scaled * hat, axis=-1, keepdims=True))


def split3(v):
    hi = v.astype(BF).astype(F32)
    mid = (v - hi).astype(BF).astype(F32)
    return hi, mid, v - hi - mid


def layer(cfg, *refs):
    nc, nf, p, plans = cfg["nc"], cfg["nf"], cfg["p"], cfg["plans"]
    names = cfg["names"]
    R = dict(zip(names, refs, strict=True))
    x, cot, vec, lens = R["x"], R["cot"], R["vec"], R["lens"]
    wq_s, wo_s, wu_s, wd_s = R["wq_s"], R["wo_s"], R["wu_s"], R["wd_s"]
    wl, wo, wu, wd = R["wl"], R["wo"], R["wu"], R["wd"]
    vsum, bu = R["vsum"], R["bu"]
    xg, h1g, qp, kp, vp, of = R["xg"], R["h1g"], R["qp"], R["kp"], R["vp"], R["of"]
    omsg, oin, o2, res, h2, gb, gh = R["omsg"], R["oin"], R["o2"], R["res"], R["h2"], R["gb"], R["gh"]
    c, f = lax.axis_index("ctx"), lax.axis_index("fsdp")
    qs = nc // GROUPS
    g, m = c // qs, c % qs
    rows, D = x.shape
    T = rows // 2
    FF = wu.shape[1]
    core = c % 2
    sib = flip(c, 1)
    top = g // 4
    gq = g % 4
    odd = (gq % 2) == 1
    gf = flip(g, 4)
    far = flip(c, nc // 2)
    NQ = GROUPS * T
    NK = NQ * qs
    lsem = R["lsem"]
    wire = Wire(R["send"], R["recv"], f)

    done = set()

    def ready(i):
        if i not in done:
            loads[i].wait()
            done.add(i)

    lane = lax.broadcasted_iota(jnp.int32, (T, 128), 1)
    low = lane < HDIM

    off = (3 * (gq // 2) + gq % 2) * 128
    loads = []

    def load(src, dst):
        cp = pltpu.make_async_copy(src, dst, lsem.at[len(loads)])
        cp.start()
        loads.append(cp)

    nq = wq_s.shape[0]
    wcols = [span(i * D + off, 256, 128) for i in range(3)]
    for i in range(3):
        load(wq_s.at[:, wcols[i]], wl.at[span(f * nq, nq), i * 256 : (i + 1) * 256])
    for s, w in ((wo_s, wo), (wu_s, wu), (wd_s, wd)):
        load(s, w.at[span(f * s.shape[0], s.shape[0])])

    barrier = pltpu.get_barrier_semaphore()
    mates = [(((g + k) % GROUPS) * qs + m, f) for k in range(1, GROUPS)]
    mates += [(g * qs + (m + k) % qs, f) for k in range(1, qs)]
    mates += [(c, (f + k) % nf) for k in range(1, nf)]
    for mate in mates:
        pl.semaphore_signal(barrier, inc=1, device_id=mate, device_id_type=MESH)
    pl.semaphore_wait(barrier, len(mates))

    own_rows, other_rows = span(top * T, T), span((1 - top) * T, T)
    to_far = wire.copy(x.at[other_rows], xg.at[g], far, landing=xg.at[gf]).start()
    near = [(top * 4 + (gq + k) % 4, top * 4 + (gq + 4 - k) % 4) for k in (1, 2, 3)]
    own_out = [wire.copy(x.at[own_rows], xg.at[g], t * qs + m, landing=xg.at[s]).start() for t, s in near]
    far_out = [wire.copy(xg.at[gf], xg.at[gf], t * qs + m, landing=xg.at[flip(s, 4)]) for t, s in near]
    wq_out, vec_out = [], []
    for d in range(1, nf):
        fs = (f + nf - d) % nf
        vec_out.append(wire.copy(vec, R["vin"].at[f], c, (f + d) % nf, landing=R["vin"].at[fs]).start())
        for i in range(3):
            cols = slice(i * 256, (i + 1) * 256)
            wq_out.append(wire.copy(wq_s.at[:, wcols[i]], wl.at[span(f * nq, nq), cols], c, (f + d) % nf,
                                    landing=wl.at[span(fs * nq, nq), cols]).start())
    weights = [Gather(wire, c, f, nf, p, s, w) for s, w in ((wo_s, wo), (wu_s, wu), (wd_s, wd))]
    for w in weights:
        w.begin()
    to_far.arrive()
    for copy in far_out:
        copy.start()
    xg[g] = x[own_rows, :]
    vin = R["vin"]
    vin[f] = vec[...]
    for copy in vec_out:
        copy.arrive()
    vsum[...] = jnp.concatenate([vin[j].astype(F32) for j in range(nf)], axis=1)
    nv = vec.shape[1]
    bu[...] = jnp.concatenate([vsum[8 + i : 9 + i, j * nv : (j + 1) * nv] for j in range(nf) for i in range(FF // D)], axis=1)
    for mb in range(2):
        pos = c * T + lax.broadcasted_iota(jnp.int32, (T, D), 0)
        live = pos < lens[mb]
        gb[mb * T : (mb + 1) * T, :] = jnp.where(live, cot[mb * T : (mb + 1) * T, :].astype(F32), 0.0).astype(BF)
    hd = D // 2
    mine, theirs = span(core * hd, hd, 128), span((1 - core) * hd, hd, 128)
    gh[0:rows, :] = gb[:, mine]
    lower, upper = slice(0, rows), slice(rows, 2 * rows)
    g_out = wire.copy(gb.at[:, theirs], gh.at[upper], sib).start()

    for i in range(3):
        ready(i)
    for copy in wq_out:
        copy.arrive()
    length = jnp.where(top == 0, lens[0], lens[1])
    kaug_hi = jnp.where((lane >= 64) & (lane < 68), 1.0, 0.0)
    kaug_lo = jnp.where(lane < 4, 1.0, 0.0)
    vaug_hi = jnp.where((lane >= 64) & (lane < 67), 1.0, 0.0)
    vaug_lo = jnp.where(lane < 3, 1.0, 0.0)
    one_hi, one_lo = jnp.where(lane == 64, 1.0, 0.0), jnp.where(lane == 0, 1.0, 0.0)
    bias_q = vsum[2:3, span(off, 256, 128)]
    bias_v = vsum[3:4, span(off, 256, 128)]

    def pick(t0, t1):
        return jnp.where(odd, t1, t0), jnp.where(odd, pltpu.roll(t0, HDIM, 1), t1)

    def project(s):
        hat, _ = norm_rows(xg[s].astype(F32))
        h1 = (hat * vsum[0:1, :] + vsum[1:2, :]).astype(BF)
        qrows = span(s * T, T, 128)
        krows = span((m * GROUPS + s) * T, T, 128)
        h1g[qrows, :] = h1
        y = dot_nn(h1, wl[...])
        q = y[:, 0:256] + bias_q
        v = y[:, 512:768] + bias_v
        qa, qc = pick(q[:, 0:128], q[:, 128:256])
        ka, kc = pick(y[:, 256:384], y[:, 384:512])
        va, vc = pick(v[:, 0:128], v[:, 128:256])
        pos = (s * qs + m) * T + lax.broadcasted_iota(jnp.int32, (T, 128), 0)
        bias = jnp.where(pos < length, 0.0, -1e30)
        k_hi = jnp.where(lane == 64, bias, kaug_hi)
        k_lo = jnp.where(lane == 0, bias, kaug_lo)
        qa, qc = qa.astype(BF).astype(F32) * 0.125, qc.astype(BF).astype(F32) * 0.125
        qp[0, qrows, :] = jnp.where(low, qa, one_hi).astype(BF)
        qp[1, qrows, :] = jnp.where(low, one_lo, qa).astype(BF)
        qp[2, qrows, :] = jnp.where(low, qc, one_hi).astype(BF)
        kp[0, krows, :] = jnp.where(low, ka, k_hi).astype(BF)
        kp[1, krows, :] = jnp.where(low, k_lo, ka).astype(BF)
        kp[2, krows, :] = jnp.where(low, kc, k_hi).astype(BF)
        vp[0, krows, :] = jnp.where(low, va, vaug_hi).astype(BF)
        vp[1, krows, :] = jnp.where(low, vaug_lo, va).astype(BF)
        vp[2, krows, :] = jnp.where(low, vc, vaug_hi).astype(BF)

    def share(first):
        out = []
        for j in range(1, qs):
            for ref in (kp, vp):
                at = lambda who: ref.at[:, span((who * GROUPS + first) * T, 4 * T, 128), :]
                out.append(wire.copy(at(m), at(m), g * qs + (m + j) % qs, landing=at((m + qs - j) % qs)).start())
        return out

    for copy in own_out:
        copy.arrive()
    pl.loop(0, 4)(lambda i: project(top * 4 + i))
    shares = share(top * 4)
    for copy in far_out:
        copy.arrive()
    pl.loop(0, 4)(lambda i: project((1 - top) * 4 + i))
    shares += share((1 - top) * 4)
    weights[0].spread()
    weights[1].spread()
    for copy in shares:
        copy.arrive()
    weights[2].spread()

    tq = cfg["tq"]
    lane_q = lax.broadcasted_iota(jnp.int32, (tq, 128), 1)

    def attend(h):
        base = 0 if h == 1 else HDIM

        @pl.loop(0, NQ // tq)
        def _(i):
            at = span(i * tq, tq, 128)
            q = qp[h, at, :]
            s = dot_nt(q, kp[h])
            peak = jnp.max(s, axis=1, keepdims=True)
            e = jnp.exp(s - peak).astype(BF)
            o = dot_nn(e, vp[h])
            l = o[:, base : base + 1]
            of[h, at, :] = o / l
            a, b, d = split3(-(peak + jnp.log(l)))
            q = q.astype(F32)
            q = jnp.where(lane_q == base + 1, a, jnp.where(lane_q == base + 2, b, jnp.where(lane_q == base + 3, d, q)))
            qp[h, at, :] = q.astype(BF)

    def deal(msg, box, half):
        box[half, g] = msg[half, g]
        out = []
        for k in range(1, GROUPS):
            t, s = (g + k) % GROUPS, (g + GROUPS - k) % GROUPS
            out.append(wire.copy(msg.at[half, t], box.at[half, g], t * qs + m, landing=box.at[half, s]).start())
        return out

    attend(0)
    attend(1)

    @pl.loop(0, GROUPS)
    def _(s):
        at = span(s * T, T, 128)
        omsg[0, s] = jnp.where(low, of[0, at, :], of[1, at, :]).astype(BF)

    o_out = deal(omsg, oin, 0)
    weights[0].pass_on()
    attend(2)

    @pl.loop(0, GROUPS)
    def _(s):
        omsg[1, s] = of[2, span(s * T, T, 128), :].astype(BF)

    o_out += deal(omsg, oin, 1)
    weights[1].pass_on()
    weights[2].pass_on()
    for copy in o_out:
        copy.arrive()

    def tiles(jp):
        return [slice((3 * jp + i) * 128, (3 * jp + i + 1) * 128) for i in range(3)]

    for mb in range(2):
        for jp in range(2):
            g0 = 4 * mb + 2 * jp
            at = slice(mb * T, (mb + 1) * T)
            t0, t1, t2 = tiles(jp)
            o2[at, t0] = oin[0, g0]
            o2[at, t1] = jnp.where(low, oin[1, g0].astype(F32), pltpu.roll(oin[1, g0 + 1].astype(F32), HDIM, 1)).astype(BF)
            o2[at, t2] = oin[0, g0 + 1]
    o_pair = wire.copy(o2.at[lower], o2.at[upper], sib).start()
    ready(3)
    weights[0].finish()
    res[...] = x[...].astype(F32) + dot_nn(o2[lower, :], wo[...]) + vsum[4:5, :]
    hat2, _ = norm_rows(res[...])
    h2[lower, :] = (hat2 * vsum[5:6, :] + vsum[6:7, :]).astype(BF)
    h_pair = wire.copy(h2.at[lower], h2.at[upper], sib).start()
    for i in (1, 2):
        ready(3 + i)
        weights[i].finish()

    a2, duh, dus, dbu, acc, dh2 = R["a2"], R["duh"], R["dus"], R["dbu"], R["acc"], R["dh2"]
    acc[...] = jnp.zeros_like(acc)
    dh2[...] = jnp.zeros_like(dh2)
    hf = FF // 2

    def hidden(which, keep):
        @pl.loop(0, hf // WIDE)
        def _(i):
            col = which * hf + i * WIDE
            cols = span(col, WIDE, 128)
            u = dot_nn(h2[lower, :], wu[:, cols]) + bu[:, cols]
            phi = 0.5 + 0.5 * lax.erf(u * 0.7071067811865476)
            a = (u * phi).astype(BF)
            a2[lower, cols] = a
            da = dot_nt(gb[...], wd[span(col, WIDE, 128), :])
            slope = phi + u * (0.3989422804014327 * jnp.exp(-0.5 * u * u))
            du = (da * slope).astype(BF)
            keep[0:rows, span(i * WIDE, WIDE, 128)] = du
            dbu[:, cols] = jnp.sum(du.astype(F32), axis=0, keepdims=True)
            acc[...] += dot_nn(a, wd[span(col, WIDE, 128), :])
            dh2[...] += dot_nt(du, wu[:, cols])

    hidden(1 - core, dus)
    du_pair = wire.copy(dus, duh.at[upper], sib).start()
    half_cols = lambda which: span(which * hf, hf, 128)
    a_pair = [wire.copy(a2.at[lower, half_cols(1 - core)], a2.at[upper, half_cols(1 - core)], sib, landing=a2.at[upper, half_cols(core)]).start()]
    hidden(core, duh)
    a_pair.append(wire.copy(a2.at[lower, half_cols(core)], a2.at[upper, half_cols(core)], sib, landing=a2.at[upper, half_cols(1 - core)]).start())
    R["out"][...] = (res[...] + acc[...] + vsum[7:8, :]).astype(BF)
    plan = Planner()
    a_here = plan.ship({"core": 5.0})
    dr, dbh, dbs, dmsg, doin = R["dr"], R["dbh"], R["dbs"], omsg, R["doin"]
    dvb = R["dvb"]
    gd, gu, go, gqr = wd.at[:, 0:hd], wu.at[:, 0:hf], wo.at[:, 0:hd], wu.at[:, hf : hf + D]

    def residual_back():
        hat2, rstd2 = norm_rows(res[...])
        dvb[0, 5:6, :] = jnp.sum(dh2[...] * hat2, axis=0, keepdims=True)
        dvb[0, 6:7, :] = jnp.sum(dh2[...], axis=0, keepdims=True)
        dr[...] = gb[...].astype(F32) + norm_back(dh2[...], hat2, rstd2, vsum[5:6, :])
        db = dr[...].astype(BF)
        dbs[...] = db
        dvb[0, 4:5, :] = jnp.sum(db.astype(F32), axis=0, keepdims=True)
        dvb[0, 7:8, :] = jnp.sum(gb[...].astype(F32), axis=0, keepdims=True)
        dbh[0:rows, :] = dbs[:, mine]
        db_pair = wire.copy(dbs.at[:, theirs], dbh.at[upper], sib).start()
        acc[...] = dot_nt(db, wo[...])
        wire.drain(o_out)
        for t in range(GROUPS):
            mb, jj = t // 4, t % 4
            at = slice(mb * T, (mb + 1) * T)
            t0, t1, t2 = tiles(jj // 2)
            dmsg[0, t] = acc[at, t2 if jj % 2 else t0].astype(BF)
            single = acc[at, t1]
            dmsg[1, t] = (pltpu.roll(single, HDIM, 1) if jj % 2 else single).astype(BF)
        do_out = [deal(dmsg, doin, 0), deal(dmsg, doin, 1)]
        load = {"x": 2.7, "z": 4.0, "mid": 5.4}
        here = [plan.ship(load), plan.ship(load)]
        for w in weights:
            for copies in [w.a] + w.b + w.z:
                wire.drain(copies)
        wire.drain(far_out)
        return db_pair, do_out, here

    db_pair, do_out, do_here = plan.compute(2.0, residual_back)

    def shard(ref, half, c0, c1, lead=()):
        return lambda lo, n: ref.at[lead + (span(lo, n), span(core * half + c0, c1 - c0, 128))]

    lone = []

    def sibling(ref, half, c0, c1):
        def go():
            at = lambda which: ref.at[:, span(which * half + c0, c1 - c0, 128)]
            copy = wire.copy(at(core), at(core), sib, landing=at(1 - core)).start()
            plan.later(plan.ship({"core": 1.0}), copy.arrive)
        return go

    def reduction(k, j, grad, ref, half, c0, c1):
        boxes = [R[f"box_{k}{j}{i}"] for i in range(len(plans[k]))]
        Reduce(wire, plan, c, f, nf, grad.at[:, c0:c1], boxes, plans[k], shard(ref, half, c0, c1), sibling(ref, half, c0, c1),
               lsem.at[7 + len(lone)]).send()
        lone.append(k)

    def down_grads():
        for copy in a_pair:
            copy.arrive()
        g_out.arrive()

        @pl.loop(0, FF // WIDE)
        def _(i):
            at = span(i * WIDE, WIDE, 128)
            wd[at, 0:hd] = dot_tn(a2[:, at], gh[...]).astype(BF)

        for j, (c0, c1) in enumerate(cfg["cuts"]["d"]):
            reduction("d", j, gd, R["fd"], hd, c0, c1)

    plan.compute(2.0, down_grads, a_here)

    def up_grads():
        h_pair.arrive()
        du_pair.arrive()
        for j, (c0, c1) in enumerate(cfg["cuts"]["u"]):
            wu[:, c0:c1] = dot_tn(h2[...], duh[:, c0:c1]).astype(BF)
            reduction("u", j, gu, R["fu"], hf, c0, c1)

    plan.compute(2.2, up_grads)

    def out_grads():
        o_pair.arrive()
        db_pair.arrive()
        wo[:, 0:hd] = dot_tn(o2[...], dbh[...]).astype(BF)
        for j, (c0, c1) in enumerate(cfg["cuts"]["o"]):
            reduction("o", j, go, R["fo"], hd, c0, c1)

    plan.compute(0.7, out_grads)

    dop, dka, dva, dkv, dkvin, dqkv = (R[k] for k in ("dop", "dka", "dva", "dkv", "dkvin", "dqkv"))
    dqa = of
    tb, kc = cfg["tb"], cfg["kc"]
    lane_b = lax.broadcasted_iota(jnp.int32, (tb, 128), 1)

    def prepare(h):
        half = 1 if h == 2 else 0
        base = 0 if h == 1 else HDIM

        @pl.loop(0, GROUPS)
        def _(s):
            at = span(s * T, T, 128)
            d = doin[half, s].astype(F32)
            d = jnp.where(low, 0.0, d) if h == 1 else jnp.where(low, d, 0.0)
            a, b, e = split3(-jnp.sum(d * of[h, at, :], axis=1, keepdims=True))
            d = jnp.where(lane == base, a, jnp.where(lane == base + 1, b, jnp.where(lane == base + 2, e, d)))
            dop[h, at, :] = d.astype(BF)

    def retrace(h, first, last):
        keep = (lambda v: jnp.where(lane_b < HDIM, 0.0, v)) if h == 1 else (lambda v: jnp.where(lane_b < HDIM, v, 0.0))
        if h != 1 and first == 0:
            dka[...] = jnp.zeros((NK, 128), F32)
            dva[...] = jnp.zeros((NK, 128), F32)

        @pl.loop(first, last)
        def _(i):
            at = span(i * tb, tb, 128)
            q, d = qp[h, at, :], dop[h, at, :]
            q0, d0 = keep(q.astype(F32)).astype(BF), keep(d.astype(F32)).astype(BF)
            dq = jnp.zeros((tb, 128), F32)
            for j in range(NK // kc):
                ks = slice(j * kc, (j + 1) * kc)
                k, v = kp[h, ks, :], vp[h, ks, :]
                pt = jnp.exp(dot_nt(k, q))
                ds = (pt * dot_nt(v, d)).astype(BF)
                dva[ks, :] += dot_nn(pt.astype(BF), d0)
                dka[ks, :] += dot_nn(ds, q0)
                dq = dq + dot_tn(ds, k)
            dqa[h, at, :] = dq * 0.125

    def trade(half):
        out = []
        for j in range(1, qs):
            part = (m + j) % qs

            @pl.loop(0, GROUPS)
            def _(s):
                at = span((part * GROUPS + s) * T, T, 128)
                to = span(s * T, T, 128)
                dkv[j - 1, 0, to, :] = dka[at, :].astype(BF)
                dkv[j - 1, 1, to, :] = dva[at, :].astype(BF)

            out.append(wire.copy(dkv.at[j - 1], dkvin.at[j - 1, half], g * qs + part).start())
        return out

    def place(half, base, at, tile):
        if half == 0:
            dqkv[at, base : base + 128] = jnp.where(odd, dqkv[at, base : base + 128].astype(F32), tile).astype(BF)
            dqkv[at, base + 128 : base + 256] = jnp.where(odd, tile, dqkv[at, base + 128 : base + 256].astype(F32)).astype(BF)
        else:
            turned = pltpu.roll(tile, HDIM, 1)
            dqkv[at, base : base + 128] = jnp.where(odd, turned, dqkv[at, base : base + 128].astype(F32)).astype(BF)
            dqkv[at, base + 128 : base + 256] = jnp.where(odd, dqkv[at, base + 128 : base + 256].astype(F32), tile).astype(BF)

    def settle_heads(half, trades):
        for copy in trades:
            copy.arrive()
        wire.drain(trades)
        pair = half == 0

        @pl.loop(0, GROUPS)
        def _(s):
            at = span(s * T, T, 128)
            mine_at = span((m * GROUPS + s) * T, T, 128)
            if pair:
                tile = jnp.where(low, dqa[0, at, :], dqa[1, at, :])
            else:
                tile = jnp.where(low, dqa[2, at, :], 0.0)
            place(half, 0, at, tile)
            for which, acc_ref in ((0, dka), (1, dva)):
                tile = acc_ref[mine_at, :]
                for j in range(1, qs):
                    tile = tile + dkvin[j - 1, half, which, at, :].astype(F32)
                place(half, 256 * (which + 1), at, tile)

    def retrace_all(h):
        n = NQ // tb
        for first, last in ((0, n // 2), (n // 2, n)):
            plan.compute(3.2, lambda: retrace(h, first, last))

    def ready_pair():
        dqkv[...] = jnp.zeros_like(dqkv)
        for copy in do_out[0]:
            copy.arrive()
        prepare(0)
        prepare(1)

    def ready_single():
        for copy in do_out[1]:
            copy.arrive()
        prepare(2)

    plan.compute(1.9, ready_pair, do_here[0])
    retrace_all(0)
    retrace_all(1)
    trades = plan.compute(0.5, lambda: trade(0))
    pair_here = plan.ship({"core": 3.0})
    plan.compute(1.0, ready_single, do_here[1])
    plan.compute(1.0, lambda: settle_heads(0, trades), pair_here)
    retrace_all(2)
    trades = plan.compute(0.5, lambda: trade(1))
    plan.compute(1.0, lambda: settle_heads(1, trades), plan.ship({"core": 3.0}))

    dh1p, dh1in, dh1, farbox = xg, R["dh1in"], dh2, R["farbox"]
    gqh, box_c = wu.at[:, hf + D : hf + D + hd], dop

    def inputs_back():
        pl.loop(0, GROUPS)(lambda s: dh1p.__setitem__(s, dot_nt(dqkv[span(s * T, T, 128), :], wl[...]).astype(BF)))
        out = [wire.copy(dh1p.at[flip(t, 4)], dh1in.at[k, 1], t * qs + m).start() for k, (t, s) in enumerate(near)]
        out += [wire.copy(dh1p.at[t], dh1in.at[k, 0], t * qs + m).start() for k, (t, s) in enumerate(near)]
        return out

    dh_out = plan.compute(2.0, inputs_back)
    dh_here = [plan.ship({"x": 8.0, "z": 8.0}), plan.ship({"x": 8.0, "z": 8.0})]

    def qkv_grads():
        for i in range(0, D, 256):
            gqr[:, i : i + 256] = dot_tn(h1g[...], dqkv[:, i : i + 256]).astype(BF)
        return [
            wire.copy(gqr.at[:, span((1 - core) * hd + i * 128, 128, 128)], box_c.at[i, 0:D], sib).start() for i in range(hd // 128)
        ]

    gq_pair = plan.compute(2.0, qkv_grads)
    gq_here = plan.ship({"core": 2.0})

    def column_sums():
        colsum = lax.fori_loop(
            0, GROUPS, lambda i, t: t + jnp.sum(dqkv[span(i * T, T, 128), :].astype(F32), axis=0, keepdims=True), jnp.zeros((1, D), F32)
        )
        dvb[0, 2:4, :] = jnp.zeros((2, D), F32)
        dvb[0, 12:16, :] = jnp.zeros((4, D), F32)
        dvb[0, 2:3, span(off, 256, 128)] = colsum[:, 0:256]
        dvb[0, 3:4, span(off, 256, 128)] = colsum[:, 512:768]
        for i in range(FF // D):
            dvb[0, 8 + i : 9 + i, :] = dbu[0:1, i * D : (i + 1) * D]

    plan.compute(0.5, column_sums)
    fq = R["fq"]

    def spread_q():
        moves = [(2, [gq]), (1, [gq, flip(gq, 2)]), (0, None)]

        def go():
            bit, have = moves.pop(0)
            if bit:
                ref = lambda jj: fq.at[jj, :, span(core * hd, hd, 128)]
                mate = flip(c, bit * qs)
                copies = [wire.copy(ref(j), ref(j), mate, landing=ref(flip(j, bit))).start() for j in have]
                us = len(have) * fq.shape[1] * hd * 4 / 98e3
            else:
                at = lambda which: fq.at[:, :, span(which * hd, hd, 128)]
                copies = [wire.copy(at(core), at(core), sib, landing=at(1 - core)).start()]
                us = 12.0

            def come():
                for copy in copies:
                    copy.arrive()
                if moves:
                    go()

            plan.later(plan.ship(road("c", 2 * bit if bit else 1, us)), come)

        go()

    def sum_q():
        for copy in gq_pair:
            copy.arrive()
        for i in range(hd // 128):
            at = slice(i * 128, (i + 1) * 128)
            gqh[:, at] = (gqr[:, span(core * hd + i * 128, 128, 128)].astype(F32) + box_c[i, 0:D].astype(F32)).astype(BF)
        Reduce(wire, plan, c, f, nf, gqh, [R[f"box_q0{i}"] for i in range(len(plans["q"]))], plans["q"],
               shard(fq, hd, 0, hd, (gq,)), spread_q, lsem.at[6]).send()

    plan.compute(0.5, sum_q, gq_here)

    def total_of(which, block):
        s = dh1p[block].astype(F32)
        for k in range(3):
            s = s + dh1in[k, which].astype(F32)
        return s

    def far_total():
        for copy in dh_out[:3]:
            copy.arrive()
        wire.drain([g_out])
        gb[0:T, :] = total_of(1, gf).astype(BF)
        return wire.copy(gb.at[0:T], farbox, far).start()

    far_back = plan.compute(0.5, far_total, dh_here[0])
    far_here = plan.ship({"z": 4.0, "mid": 8.0})

    def near_total():
        for copy in dh_out[3:]:
            copy.arrive()
        dh1[own_rows, :] = total_of(0, g)

    plan.compute(0.5, near_total, dh_here[1])
    dvin = R["dvin"]
    bits = [("c", 1 << b) for b in range(nc.bit_length() - 1)] + [("f", 1 << b) for b in range(nf.bit_length() - 1)]

    def vectors(i=0):
        if i == len(bits):
            final, own = dvb[i], jnp.zeros((16, nv), F32)
            for j in range(nf):
                own = jnp.where(f == j, final[:, j * nv : (j + 1) * nv], own)
            for r in range(FF // D):
                for j in range(nf):
                    flat = (j * (FF // D) + r) * nv
                    piece = final[8 + flat // D : 9 + flat // D, flat % D : flat % D + nv]
                    R["dvec"][8 + r : 9 + r, :] = piece if j == 0 else jnp.where(f == j, piece, R["dvec"][8 + r : 9 + r, :])
            R["dvec"][0:8, :] = own[0:8]
            R["dvec"][12:16, :] = own[12:16]
            return
        axis, bit = bits[i]
        peer = (c, flip(f, bit)) if axis == "f" else (flip(c, bit), f)
        moved = wire.copy(dvb.at[i], dvin.at[i], *peer).start()

        def come():
            moved.arrive()
            dvb[i + 1] = dvb[i] + dvin[i]
            vectors(i + 1)

        plan.later(plan.ship(road(axis, bit, 1.0)), come)

    def finish_inputs():
        far_back.arrive()
        dh1[other_rows, :] = farbox[...].astype(F32)
        hat1, rstd1 = norm_rows(x[...].astype(F32))
        dvb[0, 0:1, :] = jnp.sum(dh1[...] * hat1, axis=0, keepdims=True)
        dvb[0, 1:2, :] = jnp.sum(dh1[...], axis=0, keepdims=True)
        vectors()
        R["gin"][...] = (dr[...] + norm_back(dh1[...], hat1, rstd1, vsum[0:1, :])).astype(BF)

    plan.compute(1.7, finish_inputs, far_here)
    plan.finish()
    gq_o = R["gq"]
    nrow = fq.shape[1]
    step = next(n for n in (128, 96, 64, 48, 32, 16) if nrow % n == 0)

    @pl.loop(0, nrow // step)
    def _(i):
        at = span(i * step, step)
        for t in range(3):
            for a in range(2):
                base, src = t * D + a * 384, 256 * t
                gq_o[at, base : base + 128] = fq[2 * a, at, src : src + 128]
                shared = fq[2 * a, at, src + 128 : src + 256].astype(F32) + fq[2 * a + 1, at, src : src + 128].astype(F32)
                gq_o[at, base + 128 : base + 256] = shared.astype(BF)
                gq_o[at, base + 256 : base + 384] = fq[2 * a + 1, at, src + 128 : src + 256]

    wire.drain()


def call(nc, nf, x, cot, vec, lens, wq, wo, wu, wd):
    qs = nc // GROUPS
    R, D = x.shape
    T, FF = R // 2, wu.shape[1]
    NQ, NK = GROUPS * T, GROUPS * T * qs
    hd, hf = D // 2, FF // 2
    p = next(p for p in (8, 4, 2) if nc % p == 0 and all(w.shape[0] % (16 * p) == 0 for w in (wo, wu, wd)))
    fbits = [("f", 1 << b) for b in reversed(range(nf.bit_length() - 1))]
    cbits = [("c", 1 << b) for b in range(1, nc.bit_length() - 1)]
    qbits = [("c", 1 << b) for b in range(1, qs.bit_length() - 1)] + [("c", nc // 2)]
    plans = {"d": reduce_plan(FF, fbits + cbits), "u": reduce_plan(D, fbits + cbits), "o": reduce_plan(D, fbits + cbits),
             "q": reduce_plan(D, fbits + qbits)}
    sds, dma = jax.ShapeDtypeStruct, pltpu.SemaphoreType.DMA
    any_, vm, sm = (pl.BlockSpec(memory_space=s) for s in (pl.ANY, pltpu.VMEM, pltpu.SMEM))
    ins = ["x", "cot", "vec", "lens", "wq_s", "wo_s", "wu_s", "wd_s"]
    outs = {"out": sds((R, D), BF), "gin": sds((R, D), BF), "dvec": sds((16, D // nf), F32), "gq": sds((D // nf, 3 * D), BF),
            "fo": sds((D // nf, D), BF), "fu": sds((D // nf, FF), BF), "fd": sds((FF // nf, D), BF)}
    nb = nc.bit_length() + nf.bit_length() - 2
    b, s = (lambda *shape: pltpu.VMEM(shape, BF)), (lambda *shape: pltpu.VMEM(shape, F32))
    scratch = {
        "wl": b(D, D), "wo": b(D, D), "wu": b(D, FF), "wd": b(FF, D), "vsum": s(16, D), "bu": s(1, FF), "vin": b(nf, 16, D // nf),
        "xg": b(GROUPS, T, D), "h1g": b(NQ, D), "qp": b(3, NQ, 128), "kp": b(3, NK, 128), "vp": b(3, NK, 128), "of": s(3, NQ, 128),
        "omsg": b(2, GROUPS, T, 128), "oin": b(2, GROUPS, T, 128), "o2": b(2 * R, D), "res": s(R, D), "h2": b(2 * R, D), "gb": b(R, D),
        "gh": b(2 * R, hd), "a2": b(2 * R, FF), "duh": b(2 * R, hf), "dus": b(R, hf), "dbu": s(1, FF), "acc": s(R, D), "dh2": s(R, D),
        "dr": s(R, D), "dbh": b(2 * R, hd), "dbs": b(R, D), "doin": b(2, GROUPS, T, 128),
        "dop": b(3, NQ, 128), "dka": s(NK, 128), "dva": s(NK, 128),
        "dkv": b(qs - 1, 2, NQ, 128), "dkvin": b(qs - 1, 2, 2, NQ, 128), "dqkv": b(NQ, D),
        "dh1in": b(3, 2, T, D), "farbox": b(T, D),
        "dvb": s(nb + 1, 16, D), "dvin": s(nb, 16, D),
        "fq": b(4, D // nf, D),
        "lsem": dma((16,)), "send": dma((400,)), "recv": dma((400,)),
    }
    cuts = {"d": [(i, i + 128) for i in range(0, hd, 128)], "u": [(i, i + 512) for i in range(0, hf, 512)], "o": [(0, hd)], "q": [(0, hd)]}
    for k in cuts:
        for j, (c0, c1) in enumerate(cuts[k]):
            for i, (_, _, _, n) in enumerate(plans[k]):
                scratch[f"box_{k}{j}{i}"] = b(n, c1 - c0)
    cfg = dict(nc=nc, nf=nf, p=p, plans=plans, names=ins + list(outs) + list(scratch), cuts=cuts, tq=128, tb=256, kc=512)
    return pl.pallas_call(
        functools.partial(layer, cfg),
        out_shape=list(outs.values()),
        in_specs=[vm, vm, vm, sm, any_, any_, any_, any_],
        out_specs=[vm, vm, vm, vm, any_, any_, any_],
        scratch_shapes=list(scratch.values()),
        compiler_params=pltpu.CompilerParams(collective_id=0, has_side_effects=True, vmem_limit_bytes=62_464 * 1024),
    )(x, cot, vec, lens, wq, wo, wu, wd)


def body(inputs, cotangent, lengths, g1, b1, w_qkv, bias_q, bias_v, w_out, bias_out, g2, b2, w_up, bias_up, w_down, bias_down, nc, nf):
    MB, _, T, D = inputs.shape
    n = g1.shape[0]
    small, at, flat = [g1, b1, bias_q, bias_v, bias_out, g2, b2, bias_down, bias_up], 0, 0
    for v in small:
        flat = flat + lax.pad(v, jnp.zeros((), BF), ((at, 16 * n - at - v.shape[0], 0),))
        at += v.shape[0]
    vec = flat.reshape(16, n)
    out, gin, dvec, fq, fo, fu, fd = call(nc, nf, inputs.reshape(MB * T, D), cotangent.reshape(MB * T, D), vec, lengths[:, 0],
                                          w_qkv, w_out, w_up, w_down)
    grads = [v.astype(F32) for v in (fq, fo, fu, fd)]
    shape = (MB, 1, T, D)
    row = lambda i: dvec[i]
    return (out.reshape(shape), gin.reshape(shape), row(0), row(1), grads[0], row(2), row(3), grads[1], row(4),
            row(5), row(6), grads[2], dvec[8:12].reshape(-1), grads[3], row(7))


def solution(mesh):
    nc, nf = mesh.shape["ctx"], mesh.shape["fsdp"]
    act = P(None, "fsdp", "ctx", None)
    one, two = P("fsdp"), P("fsdp", None)
    return jax.shard_map(
        functools.partial(body, nc=nc, nf=nf),
        mesh=mesh,
        in_specs=(act, act, P(None, "fsdp"), one, one, two, one, one, two, one, one, one, two, one, two, one),
        out_specs=(act, act, one, one, two, one, one, two, one, one, one, two, one, two, one),
        check_vma=False,
    )
```

```python
import functools
import heapq

import jax
import jax.numpy as jnp
from jax import lax
from jax.experimental import pallas as pl
from jax.experimental.pallas import tpu as pltpu
from jax.sharding import PartitionSpec as P

HEADS = 12
HDIM = 64
GROUPS = 8
EPS = 1e-6
BF = jnp.bfloat16
F32 = jnp.float32
WIDE = 512
MESH = pl.DeviceIdType.MESH


def dot_nn(a, b):
    return lax.dot_general(a, b, (((1,), (0,)), ((), ())), preferred_element_type=F32)


def dot_nt(a, b):
    return lax.dot_general(a, b, (((1,), (1,)), ((), ())), preferred_element_type=F32)


def dot_tn(a, b):
    return lax.dot_general(a, b, (((0,), (0,)), ((), ())), preferred_element_type=F32)


def flip(index, bit):
    return index + bit - 2 * bit * ((index // bit) % 2)


def span(start, size, unit=16):
    return pl.ds(pl.multiple_of(start, unit), size)


class Copy:
    def __init__(self, wire, src, dst, ctx, fsdp, landing):
        self.wire, self.src, self.dst, self.landing = wire, src, dst, landing
        self.ctx, self.fsdp, self.i = ctx, fsdp, wire.count
        self.arrived = False
        wire.count += 1

    def of(self, dst):
        return pltpu.make_async_remote_copy(
            src_ref=self.src, dst_ref=dst, send_sem=self.wire.send.at[self.i], recv_sem=self.wire.recv.at[self.i],
            device_id=(self.ctx, self.fsdp), device_id_type=MESH,
        )

    def start(self):
        self.of(self.dst).start()
        self.wire.open.append(self)
        return self

    def arrive(self):
        self.of(self.landing).wait_recv()
        self.arrived = True

    def left(self):
        self.of(self.dst).wait_send()


class Wire:
    def __init__(self, send, recv, fsdp):
        self.send, self.recv, self.fsdp = send, recv, fsdp
        self.count, self.open = 0, []

    def copy(self, src, dst, ctx, fsdp=None, landing=None):
        return Copy(self, src, dst, ctx, self.fsdp if fsdp is None else fsdp, dst if landing is None else landing)

    def drain(self, copies=None):
        for copy in list(self.open) if copies is None else copies:
            copy.left()
            self.open.remove(copy)

    def finish(self):
        for copy in self.open:
            if not copy.arrived:
                copy.arrive()
        self.drain()


class Planner:
    def __init__(self):
        self.now, self.free, self.queue, self.serial = 0.0, {}, [], 0

    def ship(self, loads):
        end = self.now
        for link, us in loads.items():
            self.free[link] = max(self.now, self.free.get(link, 0.0)) + us
            end = max(end, self.free[link])
        return end + 1.5

    def later(self, when, run):
        self.serial += 1
        heapq.heappush(self.queue, (when, self.serial, run))

    def until(self, when):
        while self.queue and self.queue[0][0] <= max(self.now, when):
            at, _, run = heapq.heappop(self.queue)
            self.now = max(self.now, at)
            run()
            self.now += 0.2
        self.now = max(self.now, when)

    def compute(self, us, run, needs=0.0):
        self.until(needs)
        out = run()
        self.now += us
        return out

    def finish(self):
        self.until(1e9)


def road(axis, bit, us):
    if axis == "f":
        return {"y%d" % bit: us}
    return {1: {"core": us / 5}, 2: {"x": us}, 4: {"z": us}, 8: {"z": us, "mid": 2 * us}}.get(bit, {"far%d" % bit: us})


class Gather:
    def __init__(self, wire, c, f, nf, p, shard, full):
        rows = shard.shape[0]
        n = rows // p
        r = c % p
        self.a, self.b, self.z = [], [], []
        at = lambda owner, part: full.at[span(owner * rows + part * n, n)]
        sib = lambda i: flip(i, 1)
        for d in range(1, nf):
            fs = (f + nf - d) % nf
            self.a.append(wire.copy(shard.at[span(r * n, n)], at(f, r), c, (f + d) % nf, landing=at(fs, r)))
            near = []
            for j in range(1, p // 2):
                other, part = c, r
                for bit in (2, 4):
                    if (2 * j) & bit:
                        other, part = flip(other, bit), flip(part, bit)
                near.append((wire.copy(at(fs, r), at(fs, r), other, landing=at(fs, part)), part))
            self.b.append([copy for copy, _ in near])
            self.z.append([wire.copy(at(fs, q), at(fs, q), sib(c), landing=at(fs, sib(q))) for q in [r] + [q for _, q in near]])

    def begin(self):
        for copy in self.a:
            copy.start()

    def spread(self):
        for a, b, z in zip(self.a, self.b, self.z):
            a.arrive()
            for copy in b:
                copy.start()
            z[0].start()

    def pass_on(self):
        for b, z in zip(self.b, self.z):
            for near, sib in zip(b, z[1:]):
                near.arrive()
                sib.start()

    def finish(self):
        for z in self.z:
            for copy in z:
                copy.arrive()


def reduce_plan(rows, steps):
    plan = []
    for axis, bit in steps:
        halve = axis == "f" or rows % 32 == 0
        rows = rows // 2 if halve else rows
        plan.append((axis, bit, halve, rows))
    return plan


class Reduce:
    def __init__(self, wire, plan, c, f, nf, grad, boxes, steps, result, spread, lsem):
        self.wire, self.plan, self.c, self.f, self.grad, self.boxes, self.steps = wire, plan, c, f, grad, boxes, steps
        self.result, self.spread, self.lsem = result, spread, lsem
        self.base = f * (grad.shape[0] // nf)
        self.rows_us = 2 * 2 * grad.shape[1] / 98e3
        self.step, self.low, self.marks = 0, 0, []

    def peer(self, axis, bit):
        return (self.c, flip(self.f, bit)) if axis == "f" else (flip(self.c, bit), self.f)

    def send(self):
        if self.step == len(self.steps):
            return self.settle()
        axis, bit, halve, n = self.steps[self.step]
        mine = ((self.f if axis == "f" else self.c) // bit) % 2
        give = self.low + (1 - mine) * n if halve else self.low
        self.keep = self.low + mine * n if halve else self.low
        self.moving = self.wire.copy(self.grad.at[span(give, n)], self.boxes[self.step], *self.peer(axis, bit)).start()
        self.plan.later(self.plan.ship(road(axis, bit, n * self.rows_us)), self.add)

    def add(self):
        axis, bit, halve, n = self.steps[self.step]
        self.moving.arrive()
        box, grad, keep = self.boxes[self.step], self.grad, self.keep
        if not halve:
            self.wire.drain([self.moving])
        width = next(w for w in (128, 96, 64, 48, 32, 16) if n % w == 0)

        @pl.loop(0, n // width)
        def _(i):
            rows = span(keep + i * width, width)
            grad[rows, :] = (grad[rows, :].astype(F32) + box[span(i * width, width), :].astype(F32)).astype(BF)

        self.plan.now += n * grad.shape[1] / 4e5
        if axis == "c" and halve:
            self.marks.append((bit, keep, n))
        self.low, self.n = keep, n
        self.step += 1
        self.send()

    def settle(self):
        self.local = pltpu.make_async_copy(self.grad.at[span(self.low, self.n)], self.result(self.low - self.base, self.n), self.lsem)
        self.local.start()
        self.first = True
        self.give_back()

    def give_back(self):
        if self.local and (not self.first or not self.marks):
            self.local.wait()
            self.local = None
        if not self.marks:
            self.spread()
            return
        bit, low, n = self.marks.pop()
        mine = (self.c // bit) % 2
        there = low + n - 2 * n * mine
        src = self.grad.at[span(low, n)] if self.first else self.result(low - self.base, n)
        self.moving = self.wire.copy(src, self.result(low - self.base, n), flip(self.c, bit), landing=self.result(there - self.base, n)).start()
        self.first = False
        self.plan.later(self.plan.ship(road("c", bit, n * self.rows_us)), self.take_back)

    def take_back(self):
        self.moving.arrive()
        self.give_back()


def norm_rows(v):
    cen = v - jnp.mean(v, axis=-1, keepdims=True)
    rstd = lax.rsqrt(jnp.mean(cen * cen, axis=-1, keepdims=True) + EPS)
    return cen * rstd, rstd


def norm_back(grad, hat, rstd, gain):
    scaled = grad * gain
    return rstd * (scaled - jnp.mean(scaled, axis=-1, keepdims=True) - hat * jnp.mean(scaled * hat, axis=-1, keepdims=True))


def split3(v):
    hi = v.astype(BF).astype(F32)
    mid = (v - hi).astype(BF).astype(F32)
    return hi, mid, v - hi - mid


def layer(cfg, *refs):
    nc, nf, p, plans = cfg["nc"], cfg["nf"], cfg["p"], cfg["plans"]
    names = cfg["names"]
    R = dict(zip(names, refs, strict=True))
    x, cot, vec, lens = R["x"], R["cot"], R["vec"], R["lens"]
    wq_s, wo_s, wu_s, wd_s = R["wq_s"], R["wo_s"], R["wu_s"], R["wd_s"]
    wl, wo, wu, wd = R["wl"], R["wo"], R["wu"], R["wd"]
    vsum, bu = R["vsum"], R["bu"]
    xg, h1g, qp, kp, vp, of = R["xg"], R["h1g"], R["qp"], R["kp"], R["vp"], R["of"]
    omsg, oin, o2, res, h2, gb, gh = R["omsg"], R["oin"], R["o2"], R["res"], R["h2"], R["gb"], R["gh"]
    c, f = lax.axis_index("ctx"), lax.axis_index("fsdp")
    qs = nc // GROUPS
    g, m = c // qs, c % qs
    rows, D = x.shape
    T = rows // 2
    FF = wu.shape[1]
    core = c % 2
    sib = flip(c, 1)
    top = g // 4
    gq = g % 4
    odd = (gq % 2) == 1
    gf = flip(g, 4)
    far = flip(c, nc // 2)
    NQ = GROUPS * T
    NK = NQ * qs
    lsem = R["lsem"]
    wire = Wire(R["send"], R["recv"], f)

    done = set()

    def ready(i):
        if i not in done:
            loads[i].wait()
            done.add(i)

    lane = lax.broadcasted_iota(jnp.int32, (T, 128), 1)
    low = lane < HDIM

    off = (3 * (gq // 2) + gq % 2) * 128
    loads = []

    def load(src, dst):
        cp = pltpu.make_async_copy(src, dst, lsem.at[len(loads)])
        cp.start()
        loads.append(cp)

    nq = wq_s.shape[0]
    wcols = [span(i * D + off, 256, 128) for i in range(3)]
    for i in range(3):
        load(wq_s.at[:, wcols[i]], wl.at[span(f * nq, nq), i * 256 : (i + 1) * 256])
    for s, w in ((wo_s, wo), (wu_s, wu), (wd_s, wd)):
        load(s, w.at[span(f * s.shape[0], s.shape[0])])

    barrier = pltpu.get_barrier_semaphore()
    mates = [(((g + k) % GROUPS) * qs + m, f) for k in range(1, GROUPS)]
    mates += [(g * qs + (m + k) % qs, f) for k in range(1, qs)]
    mates += [(c, (f + k) % nf) for k in range(1, nf)]
    for mate in mates:
        pl.semaphore_signal(barrier, inc=1, device_id=mate, device_id_type=MESH)
    pl.semaphore_wait(barrier, len(mates))

    own_rows, other_rows = span(top * T, T), span((1 - top) * T, T)
    to_far = wire.copy(x.at[other_rows], xg.at[g], far, landing=xg.at[gf]).start()
    near = [(top * 4 + (gq + k) % 4, top * 4 + (gq + 4 - k) % 4) for k in (1, 2, 3)]
    own_out = [wire.copy(x.at[own_rows], xg.at[g], t * qs + m, landing=xg.at[s]).start() for t, s in near]
    far_out = [wire.copy(xg.at[gf], xg.at[gf], t * qs + m, landing=xg.at[flip(s, 4)]) for t, s in near]
    wq_out, vec_out = [], []
    for d in range(1, nf):
        fs = (f + nf - d) % nf
        vec_out.append(wire.copy(vec, R["vin"].at[f], c, (f + d) % nf, landing=R["vin"].at[fs]).start())
        for i in range(3):
            cols = slice(i * 256, (i + 1) * 256)
            wq_out.append(wire.copy(wq_s.at[:, wcols[i]], wl.at[span(f * nq, nq), cols], c, (f + d) % nf,
                                    landing=wl.at[span(fs * nq, nq), cols]).start())
    weights = [Gather(wire, c, f, nf, n, s, w) for n, s, w in ((p, wo_s, wo), (p, wu_s, wu), (min(p, 4), wd_s, wd))]
    for w in weights:
        w.begin()
    to_far.arrive()
    for copy in far_out:
        copy.start()
    xg[g] = x[own_rows, :]
    vin = R["vin"]
    vin[f] = vec[...]
    for copy in vec_out:
        copy.arrive()
    vsum[...] = jnp.concatenate([vin[j].astype(F32) for j in range(nf)], axis=1)
    nv = vec.shape[1]
    bu[...] = jnp.concatenate([vsum[8 + i : 9 + i, j * nv : (j + 1) * nv] for j in range(nf) for i in range(FF // D)], axis=1)
    for mb in range(2):
        pos = c * T + lax.broadcasted_iota(jnp.int32, (T, D), 0)
        live = pos < lens[mb]
        gb[mb * T : (mb + 1) * T, :] = jnp.where(live, cot[mb * T : (mb + 1) * T, :].astype(F32), 0.0).astype(BF)
    hd = D // 2
    mine, theirs = span(core * hd, hd, 128), span((1 - core) * hd, hd, 128)
    gh[0:rows, :] = gb[:, mine]
    lower, upper = slice(0, rows), slice(rows, 2 * rows)
    g_out = wire.copy(gb.at[:, theirs], gh.at[upper], sib).start()

    for i in range(3):
        ready(i)
    for copy in wq_out:
        copy.arrive()
    length = jnp.where(top == 0, lens[0], lens[1])
    kaug_hi = jnp.where((lane >= 64) & (lane < 68), 1.0, 0.0)
    kaug_lo = jnp.where(lane < 4, 1.0, 0.0)
    vaug_hi = jnp.where((lane >= 64) & (lane < 67), 1.0, 0.0)
    vaug_lo = jnp.where(lane < 3, 1.0, 0.0)
    one_hi, one_lo = jnp.where(lane == 64, 1.0, 0.0), jnp.where(lane == 0, 1.0, 0.0)
    bias_q = vsum[2:3, span(off, 256, 128)]
    bias_v = vsum[3:4, span(off, 256, 128)]

    def pick(t0, t1):
        return jnp.where(odd, t1, t0), jnp.where(odd, pltpu.roll(t0, HDIM, 1), t1)

    def project(s):
        hat, _ = norm_rows(xg[s].astype(F32))
        h1 = (hat * vsum[0:1, :] + vsum[1:2, :]).astype(BF)
        qrows = span(s * T, T, 128)
        krows = span((m * GROUPS + s) * T, T, 128)
        h1g[qrows, :] = h1
        y = dot_nn(h1, wl[...])
        q = y[:, 0:256] + bias_q
        v = y[:, 512:768] + bias_v
        qa, qc = pick(q[:, 0:128], q[:, 128:256])
        ka, kc = pick(y[:, 256:384], y[:, 384:512])
        va, vc = pick(v[:, 0:128], v[:, 128:256])
        pos = (s * qs + m) * T + lax.broadcasted_iota(jnp.int32, (T, 128), 0)
        bias = jnp.where(pos < length, 0.0, -1e30)
        k_hi = jnp.where(lane == 64, bias, kaug_hi)
        k_lo = jnp.where(lane == 0, bias, kaug_lo)
        qa, qc = qa.astype(BF).astype(F32) * 0.125, qc.astype(BF).astype(F32) * 0.125
        qp[0, qrows, :] = jnp.where(low, qa, one_hi).astype(BF)
        qp[1, qrows, :] = jnp.where(low, one_lo, qa).astype(BF)
        qp[2, qrows, :] = jnp.where(low, qc, one_hi).astype(BF)
        kp[0, krows, :] = jnp.where(low, ka, k_hi).astype(BF)
        kp[1, krows, :] = jnp.where(low, k_lo, ka).astype(BF)
        kp[2, krows, :] = jnp.where(low, kc, k_hi).astype(BF)
        vp[0, krows, :] = jnp.where(low, va, vaug_hi).astype(BF)
        vp[1, krows, :] = jnp.where(low, vaug_lo, va).astype(BF)
        vp[2, krows, :] = jnp.where(low, vc, vaug_hi).astype(BF)

    def share(first):
        out = []
        for j in range(1, qs):
            for ref in (kp, vp):
                at = lambda who: ref.at[:, span((who * GROUPS + first) * T, 4 * T, 128), :]
                out.append(wire.copy(at(m), at(m), g * qs + (m + j) % qs, landing=at((m + qs - j) % qs)).start())
        return out

    for copy in own_out:
        copy.arrive()
    pl.loop(0, 4)(lambda i: project(top * 4 + i))
    shares = share(top * 4)
    for copy in far_out:
        copy.arrive()
    pl.loop(0, 4)(lambda i: project((1 - top) * 4 + i))
    shares += share((1 - top) * 4)
    weights[0].spread()
    weights[1].spread()
    for copy in shares:
        copy.arrive()
    weights[2].spread()

    tq = cfg["tq"]
    lane_q = lax.broadcasted_iota(jnp.int32, (tq, 128), 1)

    def attend(h):
        base = 0 if h == 1 else HDIM

        @pl.loop(0, NQ // tq)
        def _(i):
            at = span(i * tq, tq, 128)
            q = qp[h, at, :]
            s = dot_nt(q, kp[h])
            peak = jnp.max(s, axis=1, keepdims=True)
            e = jnp.exp(s - peak).astype(BF)
            o = dot_nn(e, vp[h])
            l = o[:, base : base + 1]
            of[h, at, :] = o / l
            a, b, d = split3(-(peak + jnp.log(l)))
            q = q.astype(F32)
            q = jnp.where(lane_q == base + 1, a, jnp.where(lane_q == base + 2, b, jnp.where(lane_q == base + 3, d, q)))
            qp[h, at, :] = q.astype(BF)

    def deal(msg, box, half):
        box[half, g] = msg[half, g]
        out = []
        for k in range(1, GROUPS):
            t, s = (g + k) % GROUPS, (g + GROUPS - k) % GROUPS
            out.append(wire.copy(msg.at[half, t], box.at[half, g], t * qs + m, landing=box.at[half, s]).start())
        return out

    attend(0)
    attend(1)

    @pl.loop(0, GROUPS)
    def _(s):
        at = span(s * T, T, 128)
        omsg[0, s] = jnp.where(low, of[0, at, :], of[1, at, :]).astype(BF)

    o_out = deal(omsg, oin, 0)
    weights[0].pass_on()
    attend(2)

    @pl.loop(0, GROUPS)
    def _(s):
        omsg[1, s] = of[2, span(s * T, T, 128), :].astype(BF)

    o_out += deal(omsg, oin, 1)
    weights[1].pass_on()
    weights[2].pass_on()
    for copy in o_out:
        copy.arrive()

    def tiles(jp):
        return [slice((3 * jp + i) * 128, (3 * jp + i + 1) * 128) for i in range(3)]

    for mb in range(2):
        for jp in range(2):
            g0 = 4 * mb + 2 * jp
            at = slice(mb * T, (mb + 1) * T)
            t0, t1, t2 = tiles(jp)
            o2[at, t0] = oin[0, g0]
            o2[at, t1] = jnp.where(low, oin[1, g0].astype(F32), pltpu.roll(oin[1, g0 + 1].astype(F32), HDIM, 1)).astype(BF)
            o2[at, t2] = oin[0, g0 + 1]
    o_pair = wire.copy(o2.at[lower], o2.at[upper], sib).start()
    ready(3)
    weights[0].finish()
    res[...] = x[...].astype(F32) + dot_nn(o2[lower, :], wo[...]) + vsum[4:5, :]
    hat2, _ = norm_rows(res[...])
    h2[lower, :] = (hat2 * vsum[5:6, :] + vsum[6:7, :]).astype(BF)
    h_pair = wire.copy(h2.at[lower], h2.at[upper], sib).start()
    for i in (1, 2):
        ready(3 + i)
        weights[i].finish()

    a2, duh, dus, dbu, acc, dh2 = R["a2"], R["duh"], R["dus"], R["dbu"], R["acc"], R["dh2"]
    acc[...] = jnp.zeros_like(acc)
    dh2[...] = jnp.zeros_like(dh2)
    hf = FF // 2

    def hidden(which, keep):
        @pl.loop(0, hf // WIDE)
        def _(i):
            col = which * hf + i * WIDE
            cols = span(col, WIDE, 128)
            u = dot_nn(h2[lower, :], wu[:, cols]) + bu[:, cols]
            phi = 0.5 + 0.5 * lax.erf(u * 0.7071067811865476)
            a = (u * phi).astype(BF)
            a2[lower, cols] = a
            da = dot_nt(gb[...], wd[span(col, WIDE, 128), :])
            slope = phi + u * (0.3989422804014327 * jnp.exp(-0.5 * u * u))
            du = (da * slope).astype(BF)
            keep[0:rows, span(i * WIDE, WIDE, 128)] = du
            dbu[:, cols] = jnp.sum(du.astype(F32), axis=0, keepdims=True)
            acc[...] += dot_nn(a, wd[span(col, WIDE, 128), :])
            dh2[...] += dot_nt(du, wu[:, cols])

    hidden(1 - core, dus)
    du_pair = wire.copy(dus, duh.at[upper], sib).start()
    half_cols = lambda which: span(which * hf, hf, 128)
    a_pair = [wire.copy(a2.at[lower, half_cols(1 - core)], a2.at[upper, half_cols(1 - core)], sib, landing=a2.at[upper, half_cols(core)]).start()]
    hidden(core, duh)
    a_pair.append(wire.copy(a2.at[lower, half_cols(core)], a2.at[upper, half_cols(core)], sib, landing=a2.at[upper, half_cols(1 - core)]).start())
    R["out"][...] = (res[...] + acc[...] + vsum[7:8, :]).astype(BF)
    plan = Planner()
    a_here = plan.ship({"core": 5.0})
    dr, dbh, dbs, dmsg, doin = R["dr"], R["dbh"], R["dbs"], omsg, R["doin"]
    dvb = R["dvb"]
    gd, gu, go, gqr = wd.at[:, 0:hd], wu.at[:, 0:hf], wo.at[:, 0:hd], wu.at[:, hf : hf + D]

    def residual_back():
        hat2, rstd2 = norm_rows(res[...])
        dvb[0, 5:6, :] = jnp.sum(dh2[...] * hat2, axis=0, keepdims=True)
        dvb[0, 6:7, :] = jnp.sum(dh2[...], axis=0, keepdims=True)
        dr[...] = gb[...].astype(F32) + norm_back(dh2[...], hat2, rstd2, vsum[5:6, :])
        db = dr[...].astype(BF)
        dbs[...] = db
        dvb[0, 4:5, :] = jnp.sum(db.astype(F32), axis=0, keepdims=True)
        dvb[0, 7:8, :] = jnp.sum(gb[...].astype(F32), axis=0, keepdims=True)
        dbh[0:rows, :] = dbs[:, mine]
        db_pair = wire.copy(dbs.at[:, theirs], dbh.at[upper], sib).start()
        acc[...] = dot_nt(db, wo[...])
        wire.drain(o_out)
        for t in range(GROUPS):
            mb, jj = t // 4, t % 4
            at = slice(mb * T, (mb + 1) * T)
            t0, t1, t2 = tiles(jj // 2)
            dmsg[0, t] = acc[at, t2 if jj % 2 else t0].astype(BF)
            single = acc[at, t1]
            dmsg[1, t] = (pltpu.roll(single, HDIM, 1) if jj % 2 else single).astype(BF)
        do_out = [deal(dmsg, doin, 0), deal(dmsg, doin, 1)]
        load = {"x": 2.7, "z": 4.0, "mid": 5.4}
        here = [plan.ship(load), plan.ship(load)]
        for w in weights:
            for copies in [w.a] + w.b + w.z:
                wire.drain(copies)
        wire.drain(far_out)
        return db_pair, do_out, here

    db_pair, do_out, do_here = plan.compute(2.0, residual_back)

    def shard(ref, half, c0, c1, lead=()):
        return lambda lo, n: ref.at[lead + (span(lo, n), span(core * half + c0, c1 - c0, 128))]

    lone = []

    def sibling(ref, half, c0, c1):
        def go():
            at = lambda which: ref.at[:, span(which * half + c0, c1 - c0, 128)]
            copy = wire.copy(at(core), at(core), sib, landing=at(1 - core)).start()
            plan.later(plan.ship({"core": 1.0}), copy.arrive)
        return go

    def reduction(k, j, grad, ref, half, c0, c1):
        boxes = [R[f"box_{k}{j}{i}"] for i in range(len(plans[k]))]
        Reduce(wire, plan, c, f, nf, grad.at[:, c0:c1], boxes, plans[k], shard(ref, half, c0, c1), sibling(ref, half, c0, c1),
               lsem.at[7 + len(lone)]).send()
        lone.append(k)

    def down_grads():
        for copy in a_pair:
            copy.arrive()
        g_out.arrive()

        @pl.loop(0, FF // WIDE)
        def _(i):
            at = span(i * WIDE, WIDE, 128)
            wd[at, 0:hd] = dot_tn(a2[:, at], gh[...]).astype(BF)

        for j, (c0, c1) in enumerate(cfg["cuts"]["d"]):
            reduction("d", j, gd, R["fd"], hd, c0, c1)

    plan.compute(2.0, down_grads, a_here)

    def up_grads():
        h_pair.arrive()
        du_pair.arrive()
        for j, (c0, c1) in enumerate(cfg["cuts"]["u"]):
            wu[:, c0:c1] = dot_tn(h2[...], duh[:, c0:c1]).astype(BF)
            reduction("u", j, gu, R["fu"], hf, c0, c1)

    plan.compute(2.2, up_grads)

    def out_grads():
        o_pair.arrive()
        db_pair.arrive()
        wo[:, 0:hd] = dot_tn(o2[...], dbh[...]).astype(BF)
        for j, (c0, c1) in enumerate(cfg["cuts"]["o"]):
            reduction("o", j, go, R["fo"], hd, c0, c1)

    plan.compute(0.7, out_grads)

    dop, dka, dva, dkv, dkvin, dqkv = (R[k] for k in ("dop", "dka", "dva", "dkv", "dkvin", "dqkv"))
    dqa = of
    tb, kc = cfg["tb"], cfg["kc"]
    lane_b = lax.broadcasted_iota(jnp.int32, (tb, 128), 1)

    def prepare(h):
        half = 1 if h == 2 else 0
        base = 0 if h == 1 else HDIM

        @pl.loop(0, GROUPS)
        def _(s):
            at = span(s * T, T, 128)
            d = doin[half, s].astype(F32)
            d = jnp.where(low, 0.0, d) if h == 1 else jnp.where(low, d, 0.0)
            a, b, e = split3(-jnp.sum(d * of[h, at, :], axis=1, keepdims=True))
            d = jnp.where(lane == base, a, jnp.where(lane == base + 1, b, jnp.where(lane == base + 2, e, d)))
            dop[h, at, :] = d.astype(BF)

    def retrace(h, first, last):
        keep = (lambda v: jnp.where(lane_b < HDIM, 0.0, v)) if h == 1 else (lambda v: jnp.where(lane_b < HDIM, v, 0.0))
        if h != 1 and first == 0:
            dka[...] = jnp.zeros((NK, 128), F32)
            dva[...] = jnp.zeros((NK, 128), F32)

        @pl.loop(first, last)
        def _(i):
            at = span(i * tb, tb, 128)
            q, d = qp[h, at, :], dop[h, at, :]
            q0, d0 = keep(q.astype(F32)).astype(BF), keep(d.astype(F32)).astype(BF)
            dq = jnp.zeros((tb, 128), F32)
            for j in range(NK // kc):
                ks = slice(j * kc, (j + 1) * kc)
                k, v = kp[h, ks, :], vp[h, ks, :]
                pt = jnp.exp(dot_nt(k, q))
                ds = (pt * dot_nt(v, d)).astype(BF)
                dva[ks, :] += dot_nn(pt.astype(BF), d0)
                dka[ks, :] += dot_nn(ds, q0)
                dq = dq + dot_tn(ds, k)
            dqa[h, at, :] = dq * 0.125

    def trade(half):
        out = []
        for j in range(1, qs):
            part = (m + j) % qs

            @pl.loop(0, GROUPS)
            def _(s):
                at = span((part * GROUPS + s) * T, T, 128)
                to = span(s * T, T, 128)
                dkv[j - 1, 0, to, :] = dka[at, :].astype(BF)
                dkv[j - 1, 1, to, :] = dva[at, :].astype(BF)

            out.append(wire.copy(dkv.at[j - 1], dkvin.at[j - 1, half], g * qs + part).start())
        return out

    def place(half, base, at, tile):
        if half == 0:
            dqkv[at, base : base + 128] = jnp.where(odd, dqkv[at, base : base + 128].astype(F32), tile).astype(BF)
            dqkv[at, base + 128 : base + 256] = jnp.where(odd, tile, dqkv[at, base + 128 : base + 256].astype(F32)).astype(BF)
        else:
            turned = pltpu.roll(tile, HDIM, 1)
            dqkv[at, base : base + 128] = jnp.where(odd, turned, dqkv[at, base : base + 128].astype(F32)).astype(BF)
            dqkv[at, base + 128 : base + 256] = jnp.where(odd, dqkv[at, base + 128 : base + 256].astype(F32), tile).astype(BF)

    def settle_heads(half, trades):
        for copy in trades:
            copy.arrive()
        wire.drain(trades)
        pair = half == 0

        @pl.loop(0, GROUPS)
        def _(s):
            at = span(s * T, T, 128)
            mine_at = span((m * GROUPS + s) * T, T, 128)
            if pair:
                tile = jnp.where(low, dqa[0, at, :], dqa[1, at, :])
            else:
                tile = jnp.where(low, dqa[2, at, :], 0.0)
            place(half, 0, at, tile)
            for which, acc_ref in ((0, dka), (1, dva)):
                tile = acc_ref[mine_at, :]
                for j in range(1, qs):
                    tile = tile + dkvin[j - 1, half, which, at, :].astype(F32)
                place(half, 256 * (which + 1), at, tile)

    def retrace_all(h):
        n = NQ // tb
        for first, last in ((0, n // 2), (n // 2, n)):
            plan.compute(3.2, lambda: retrace(h, first, last))

    def ready_pair():
        dqkv[...] = jnp.zeros_like(dqkv)
        for copy in do_out[0]:
            copy.arrive()
        prepare(0)
        prepare(1)

    def ready_single():
        for copy in do_out[1]:
            copy.arrive()
        prepare(2)

    plan.compute(1.9, ready_pair, do_here[0])
    retrace_all(0)
    retrace_all(1)
    trades = plan.compute(0.5, lambda: trade(0))
    pair_here = plan.ship({"core": 3.0})
    plan.compute(1.0, ready_single, do_here[1])
    plan.compute(1.0, lambda: settle_heads(0, trades), pair_here)
    retrace_all(2)
    trades = plan.compute(0.5, lambda: trade(1))
    plan.compute(1.0, lambda: settle_heads(1, trades), plan.ship({"core": 3.0}))

    dh1p, dh1in, dh1, farbox = xg, R["dh1in"], dh2, R["farbox"]
    gqh, box_c = wu.at[:, hf + D : hf + D + hd], dop

    def inputs_back():
        pl.loop(0, GROUPS)(lambda s: dh1p.__setitem__(s, dot_nt(dqkv[span(s * T, T, 128), :], wl[...]).astype(BF)))
        out = [wire.copy(dh1p.at[flip(t, 4)], dh1in.at[k, 1], t * qs + m).start() for k, (t, s) in enumerate(near)]
        out += [wire.copy(dh1p.at[t], dh1in.at[k, 0], t * qs + m).start() for k, (t, s) in enumerate(near)]
        return out

    dh_out = plan.compute(2.0, inputs_back)
    dh_here = [plan.ship({"x": 8.0, "z": 8.0}), plan.ship({"x": 8.0, "z": 8.0})]

    def qkv_grads():
        for i in range(0, D, 256):
            gqr[:, i : i + 256] = dot_tn(h1g[...], dqkv[:, i : i + 256]).astype(BF)
        return [
            wire.copy(gqr.at[:, span((1 - core) * hd + i * 128, 128, 128)], box_c.at[i, 0:D], sib).start() for i in range(hd // 128)
        ]

    gq_pair = plan.compute(2.0, qkv_grads)
    gq_here = plan.ship({"core": 2.0})

    def column_sums():
        colsum = lax.fori_loop(
            0, GROUPS, lambda i, t: t + jnp.sum(dqkv[span(i * T, T, 128), :].astype(F32), axis=0, keepdims=True), jnp.zeros((1, D), F32)
        )
        dvb[0, 2:4, :] = jnp.zeros((2, D), F32)
        dvb[0, 12:16, :] = jnp.zeros((4, D), F32)
        dvb[0, 2:3, span(off, 256, 128)] = colsum[:, 0:256]
        dvb[0, 3:4, span(off, 256, 128)] = colsum[:, 512:768]
        for i in range(FF // D):
            dvb[0, 8 + i : 9 + i, :] = dbu[0:1, i * D : (i + 1) * D]

    plan.compute(0.5, column_sums)
    fq = R["fq"]

    def spread_q():
        moves = [(2, [gq]), (1, [gq, flip(gq, 2)]), (0, None)]

        def go():
            bit, have = moves.pop(0)
            if bit:
                ref = lambda jj: fq.at[jj, :, span(core * hd, hd, 128)]
                mate = flip(c, bit * qs)
                copies = [wire.copy(ref(j), ref(j), mate, landing=ref(flip(j, bit))).start() for j in have]
                us = len(have) * fq.shape[1] * hd * 4 / 98e3
            else:
                at = lambda which: fq.at[:, :, span(which * hd, hd, 128)]
                copies = [wire.copy(at(core), at(core), sib, landing=at(1 - core)).start()]
                us = 12.0

            def come():
                for copy in copies:
                    copy.arrive()
                if moves:
                    go()

            plan.later(plan.ship(road("c", 2 * bit if bit else 1, us)), come)

        go()

    def sum_q():
        for copy in gq_pair:
            copy.arrive()
        for i in range(hd // 128):
            at = slice(i * 128, (i + 1) * 128)
            gqh[:, at] = (gqr[:, span(core * hd + i * 128, 128, 128)].astype(F32) + box_c[i, 0:D].astype(F32)).astype(BF)
        Reduce(wire, plan, c, f, nf, gqh, [R[f"box_q0{i}"] for i in range(len(plans["q"]))], plans["q"],
               shard(fq, hd, 0, hd, (gq,)), spread_q, lsem.at[6]).send()

    plan.compute(0.5, sum_q, gq_here)

    def total_of(which, block):
        s = dh1p[block].astype(F32)
        for k in range(3):
            s = s + dh1in[k, which].astype(F32)
        return s

    def far_total():
        for copy in dh_out[:3]:
            copy.arrive()
        wire.drain([g_out])
        gb[0:T, :] = total_of(1, gf).astype(BF)
        return wire.copy(gb.at[0:T], farbox, far).start()

    far_back = plan.compute(0.5, far_total, dh_here[0])
    far_here = plan.ship({"z": 4.0, "mid": 8.0})

    def near_total():
        for copy in dh_out[3:]:
            copy.arrive()
        dh1[own_rows, :] = total_of(0, g)

    plan.compute(0.5, near_total, dh_here[1])
    dvin = R["dvin"]
    bits = [("c", 1 << b) for b in range(nc.bit_length() - 1)] + [("f", 1 << b) for b in range(nf.bit_length() - 1)]

    def vectors(i=0):
        if i == len(bits):
            final, own = dvb[i], jnp.zeros((16, nv), F32)
            for j in range(nf):
                own = jnp.where(f == j, final[:, j * nv : (j + 1) * nv], own)
            for r in range(FF // D):
                for j in range(nf):
                    flat = (j * (FF // D) + r) * nv
                    piece = final[8 + flat // D : 9 + flat // D, flat % D : flat % D + nv]
                    R["dvec"][8 + r : 9 + r, :] = piece if j == 0 else jnp.where(f == j, piece, R["dvec"][8 + r : 9 + r, :])
            R["dvec"][0:8, :] = own[0:8]
            R["dvec"][12:16, :] = own[12:16]
            return
        axis, bit = bits[i]
        peer = (c, flip(f, bit)) if axis == "f" else (flip(c, bit), f)
        moved = wire.copy(dvb.at[i], dvin.at[i], *peer).start()

        def come():
            moved.arrive()
            dvb[i + 1] = dvb[i] + dvin[i]
            vectors(i + 1)

        plan.later(plan.ship(road(axis, bit, 1.0)), come)

    def finish_inputs():
        far_back.arrive()
        dh1[other_rows, :] = farbox[...].astype(F32)
        hat1, rstd1 = norm_rows(x[...].astype(F32))
        dvb[0, 0:1, :] = jnp.sum(dh1[...] * hat1, axis=0, keepdims=True)
        dvb[0, 1:2, :] = jnp.sum(dh1[...], axis=0, keepdims=True)
        vectors()
        R["gin"][...] = (dr[...] + norm_back(dh1[...], hat1, rstd1, vsum[0:1, :])).astype(BF)

    plan.compute(1.7, finish_inputs, far_here)
    plan.finish()
    gq_o = R["gq"]
    nrow = fq.shape[1]
    step = next(n for n in (128, 96, 64, 48, 32, 16) if nrow % n == 0)

    @pl.loop(0, nrow // step)
    def _(i):
        at = span(i * step, step)
        for t in range(3):
            for a in range(2):
                base, src = t * D + a * 384, 256 * t
                gq_o[at, base : base + 128] = fq[2 * a, at, src : src + 128]
                shared = fq[2 * a, at, src + 128 : src + 256].astype(F32) + fq[2 * a + 1, at, src : src + 128].astype(F32)
                gq_o[at, base + 128 : base + 256] = shared.astype(BF)
                gq_o[at, base + 256 : base + 384] = fq[2 * a + 1, at, src + 128 : src + 256]

    wire.drain()


def call(nc, nf, x, cot, vec, lens, wq, wo, wu, wd):
    qs = nc // GROUPS
    R, D = x.shape
    T, FF = R // 2, wu.shape[1]
    NQ, NK = GROUPS * T, GROUPS * T * qs
    hd, hf = D // 2, FF // 2
    p = next(p for p in (8, 4, 2) if nc % p == 0 and all(w.shape[0] % (16 * p) == 0 for w in (wo, wu, wd)))
    fbits = [("f", 1 << b) for b in reversed(range(nf.bit_length() - 1))]
    cbits = [("c", 1 << b) for b in range(1, nc.bit_length() - 1)]
    qbits = [("c", 1 << b) for b in range(1, qs.bit_length() - 1)] + [("c", nc // 2)]
    plans = {"d": reduce_plan(FF, fbits + cbits), "u": reduce_plan(D, fbits + cbits), "o": reduce_plan(D, fbits + cbits),
             "q": reduce_plan(D, fbits + qbits)}
    sds, dma = jax.ShapeDtypeStruct, pltpu.SemaphoreType.DMA
    any_, vm, sm = (pl.BlockSpec(memory_space=s) for s in (pl.ANY, pltpu.VMEM, pltpu.SMEM))
    ins = ["x", "cot", "vec", "lens", "wq_s", "wo_s", "wu_s", "wd_s"]
    outs = {"out": sds((R, D), BF), "gin": sds((R, D), BF), "dvec": sds((16, D // nf), F32), "gq": sds((D // nf, 3 * D), BF),
            "fo": sds((D // nf, D), BF), "fu": sds((D // nf, FF), BF), "fd": sds((FF // nf, D), BF)}
    nb = nc.bit_length() + nf.bit_length() - 2
    b, s = (lambda *shape: pltpu.VMEM(shape, BF)), (lambda *shape: pltpu.VMEM(shape, F32))
    scratch = {
        "wl": b(D, D), "wo": b(D, D), "wu": b(D, FF), "wd": b(FF, D), "vsum": s(16, D), "bu": s(1, FF), "vin": b(nf, 16, D // nf),
        "xg": b(GROUPS, T, D), "h1g": b(NQ, D), "qp": b(3, NQ, 128), "kp": b(3, NK, 128), "vp": b(3, NK, 128), "of": s(3, NQ, 128),
        "omsg": b(2, GROUPS, T, 128), "oin": b(2, GROUPS, T, 128), "o2": b(2 * R, D), "res": s(R, D), "h2": b(2 * R, D), "gb": b(R, D),
        "gh": b(2 * R, hd), "a2": b(2 * R, FF), "duh": b(2 * R, hf), "dus": b(R, hf), "dbu": s(1, FF), "acc": s(R, D), "dh2": s(R, D),
        "dr": s(R, D), "dbh": b(2 * R, hd), "dbs": b(R, D), "doin": b(2, GROUPS, T, 128),
        "dop": b(3, NQ, 128), "dka": s(NK, 128), "dva": s(NK, 128),
        "dkv": b(qs - 1, 2, NQ, 128), "dkvin": b(qs - 1, 2, 2, NQ, 128), "dqkv": b(NQ, D),
        "dh1in": b(3, 2, T, D), "farbox": b(T, D),
        "dvb": s(nb + 1, 16, D), "dvin": s(nb, 16, D),
        "fq": b(4, D // nf, D),
        "lsem": dma((16,)), "send": dma((400,)), "recv": dma((400,)),
    }
    cuts = {"d": [(i, i + 128) for i in range(0, hd, 128)], "u": [(i, i + 512) for i in range(0, hf, 512)], "o": [(0, hd)], "q": [(0, hd)]}
    for k in cuts:
        for j, (c0, c1) in enumerate(cuts[k]):
            for i, (_, _, _, n) in enumerate(plans[k]):
                scratch[f"box_{k}{j}{i}"] = b(n, c1 - c0)
    cfg = dict(nc=nc, nf=nf, p=p, plans=plans, names=ins + list(outs) + list(scratch), cuts=cuts, tq=128, tb=256, kc=512)
    return pl.pallas_call(
        functools.partial(layer, cfg),
        out_shape=list(outs.values()),
        in_specs=[vm, vm, vm, sm, any_, any_, any_, any_],
        out_specs=[vm, vm, vm, vm, any_, any_, any_],
        scratch_shapes=list(scratch.values()),
        compiler_params=pltpu.CompilerParams(collective_id=0, has_side_effects=True, vmem_limit_bytes=62_464 * 1024),
    )(x, cot, vec, lens, wq, wo, wu, wd)


def body(inputs, cotangent, lengths, g1, b1, w_qkv, bias_q, bias_v, w_out, bias_out, g2, b2, w_up, bias_up, w_down, bias_down, nc, nf):
    MB, _, T, D = inputs.shape
    n = g1.shape[0]
    small, at, flat = [g1, b1, bias_q, bias_v, bias_out, g2, b2, bias_down, bias_up], 0, 0
    for v in small:
        flat = flat + lax.pad(v, jnp.zeros((), BF), ((at, 16 * n - at - v.shape[0], 0),))
        at += v.shape[0]
    vec = flat.reshape(16, n)
    out, gin, dvec, fq, fo, fu, fd = call(nc, nf, inputs.reshape(MB * T, D), cotangent.reshape(MB * T, D), vec, lengths[:, 0],
                                          w_qkv, w_out, w_up, w_down)
    grads = [v.astype(F32) for v in (fq, fo, fu, fd)]
    shape = (MB, 1, T, D)
    row = lambda i: dvec[i]
    return (out.reshape(shape), gin.reshape(shape), row(0), row(1), grads[0], row(2), row(3), grads[1], row(4),
            row(5), row(6), grads[2], dvec[8:12].reshape(-1), grads[3], row(7))


def solution(mesh):
    nc, nf = mesh.shape["ctx"], mesh.shape["fsdp"]
    act = P(None, "fsdp", "ctx", None)
    one, two = P("fsdp"), P("fsdp", None)
    return jax.shard_map(
        functools.partial(body, nc=nc, nf=nf),
        mesh=mesh,
        in_specs=(act, act, P(None, "fsdp"), one, one, two, one, one, two, one, one, one, two, one, two, one),
        out_specs=(act, act, one, one, two, one, one, two, one, one, one, two, one, two, one),
        check_vma=False,
    )
```

```python
import functools
import heapq

import jax
import jax.numpy as jnp
from jax import lax
from jax.experimental import pallas as pl
from jax.experimental.pallas import tpu as pltpu
from jax.sharding import PartitionSpec as P

HEADS = 12
HDIM = 64
GROUPS = 8
EPS = 1e-6
BF = jnp.bfloat16
F32 = jnp.float32
WIDE = 512
MESH = pl.DeviceIdType.MESH


def dot_nn(a, b):
    return lax.dot_general(a, b, (((1,), (0,)), ((), ())), preferred_element_type=F32)


def dot_nt(a, b):
    return lax.dot_general(a, b, (((1,), (1,)), ((), ())), preferred_element_type=F32)


def dot_tn(a, b):
    return lax.dot_general(a, b, (((0,), (0,)), ((), ())), preferred_element_type=F32)


def flip(index, bit):
    return index + bit - 2 * bit * ((index // bit) % 2)


def span(start, size, unit=16):
    return pl.ds(pl.multiple_of(start, unit), size)


class Copy:
    def __init__(self, wire, src, dst, ctx, fsdp, landing):
        self.wire, self.src, self.dst, self.landing = wire, src, dst, landing
        self.ctx, self.fsdp, self.i = ctx, fsdp, wire.count
        self.arrived = False
        wire.count += 1

    def of(self, dst):
        return pltpu.make_async_remote_copy(
            src_ref=self.src, dst_ref=dst, send_sem=self.wire.send.at[self.i], recv_sem=self.wire.recv.at[self.i],
            device_id=(self.ctx, self.fsdp), device_id_type=MESH,
        )

    def start(self):
        self.of(self.dst).start()
        self.wire.open.append(self)
        return self

    def arrive(self):
        self.of(self.landing).wait_recv()
        self.arrived = True

    def left(self):
        self.of(self.dst).wait_send()


class Wire:
    def __init__(self, send, recv, fsdp):
        self.send, self.recv, self.fsdp = send, recv, fsdp
        self.count, self.open = 0, []

    def copy(self, src, dst, ctx, fsdp=None, landing=None):
        return Copy(self, src, dst, ctx, self.fsdp if fsdp is None else fsdp, dst if landing is None else landing)

    def drain(self, copies=None):
        for copy in list(self.open) if copies is None else copies:
            copy.left()
            self.open.remove(copy)

    def finish(self):
        for copy in self.open:
            if not copy.arrived:
                copy.arrive()
        self.drain()


class Planner:
    def __init__(self):
        self.now, self.free, self.queue, self.serial = 0.0, {}, [], 0

    def ship(self, loads):
        end = self.now
        for link, us in loads.items():
            self.free[link] = max(self.now, self.free.get(link, 0.0)) + us
            end = max(end, self.free[link])
        return end + 1.5

    def later(self, when, run):
        self.serial += 1
        heapq.heappush(self.queue, (when, self.serial, run))

    def until(self, when):
        while self.queue and self.queue[0][0] <= max(self.now, when):
            at, _, run = heapq.heappop(self.queue)
            self.now = max(self.now, at)
            run()
            self.now += 0.2
        self.now = max(self.now, when)

    def compute(self, us, run, needs=0.0):
        self.until(needs)
        out = run()
        self.now += us
        return out

    def finish(self):
        self.until(1e9)


def road(axis, bit, us):
    if axis == "f":
        return {"y%d" % bit: us}
    return {1: {"core": us / 5}, 2: {"x": us}, 4: {"z": us}, 8: {"z": us, "mid": 2 * us}}.get(bit, {"far%d" % bit: us})


class Gather:
    def __init__(self, wire, c, f, nf, p, shard, full):
        rows = shard.shape[0]
        n = rows // p
        r = c % p
        self.a, self.b, self.z = [], [], []
        at = lambda owner, part: full.at[span(owner * rows + part * n, n)]
        sib = lambda i: flip(i, 1)
        for d in range(1, nf):
            fs = (f + nf - d) % nf
            self.a.append(wire.copy(shard.at[span(r * n, n)], at(f, r), c, (f + d) % nf, landing=at(fs, r)))
            near = []
            for j in range(1, p // 2):
                other, part = c, r
                for bit in (2, 4):
                    if (2 * j) & bit:
                        other, part = flip(other, bit), flip(part, bit)
                near.append((wire.copy(at(fs, r), at(fs, r), other, landing=at(fs, part)), part))
            self.b.append([copy for copy, _ in near])
            self.z.append([wire.copy(at(fs, q), at(fs, q), sib(c), landing=at(fs, sib(q))) for q in [r] + [q for _, q in near]])

    def begin(self):
        for copy in self.a:
            copy.start()

    def spread(self):
        for a, b, z in zip(self.a, self.b, self.z):
            a.arrive()
            for copy in b:
                copy.start()
            z[0].start()

    def pass_on(self):
        for b, z in zip(self.b, self.z):
            for near, sib in zip(b, z[1:]):
                near.arrive()
                sib.start()

    def finish(self):
        for z in self.z:
            for copy in z:
                copy.arrive()


def reduce_plan(rows, steps):
    plan = []
    for axis, bit in steps:
        halve = axis == "f" or rows % 32 == 0
        rows = rows // 2 if halve else rows
        plan.append((axis, bit, halve, rows))
    return plan


class Reduce:
    def __init__(self, wire, plan, c, f, nf, grad, boxes, steps, result, spread, lsem):
        self.wire, self.plan, self.c, self.f, self.grad, self.boxes, self.steps = wire, plan, c, f, grad, boxes, steps
        self.result, self.spread, self.lsem = result, spread, lsem
        self.base = f * (grad.shape[0] // nf)
        self.rows_us = 2 * 2 * grad.shape[1] / 98e3
        self.step, self.low, self.marks = 0, 0, []

    def peer(self, axis, bit):
        return (self.c, flip(self.f, bit)) if axis == "f" else (flip(self.c, bit), self.f)

    def send(self):
        if self.step == len(self.steps):
            return self.settle()
        axis, bit, halve, n = self.steps[self.step]
        mine = ((self.f if axis == "f" else self.c) // bit) % 2
        give = self.low + (1 - mine) * n if halve else self.low
        self.keep = self.low + mine * n if halve else self.low
        self.moving = self.wire.copy(self.grad.at[span(give, n)], self.boxes[self.step], *self.peer(axis, bit)).start()
        self.plan.later(self.plan.ship(road(axis, bit, n * self.rows_us)), self.add)

    def add(self):
        axis, bit, halve, n = self.steps[self.step]
        self.moving.arrive()
        box, grad, keep = self.boxes[self.step], self.grad, self.keep
        if not halve:
            self.wire.drain([self.moving])
        width = next(w for w in (128, 96, 64, 48, 32, 16) if n % w == 0)

        @pl.loop(0, n // width)
        def _(i):
            rows = span(keep + i * width, width)
            grad[rows, :] = (grad[rows, :].astype(F32) + box[span(i * width, width), :].astype(F32)).astype(BF)

        self.plan.now += n * grad.shape[1] / 4e5
        if axis == "c" and halve:
            self.marks.append((bit, keep, n))
        self.low, self.n = keep, n
        self.step += 1
        self.send()

    def settle(self):
        self.local = pltpu.make_async_copy(self.grad.at[span(self.low, self.n)], self.result(self.low - self.base, self.n), self.lsem)
        self.local.start()
        self.first = True
        self.give_back()

    def give_back(self):
        if self.local and (not self.first or not self.marks):
            self.local.wait()
            self.local = None
        if not self.marks:
            self.spread()
            return
        bit, low, n = self.marks.pop()
        mine = (self.c // bit) % 2
        there = low + n - 2 * n * mine
        src = self.grad.at[span(low, n)] if self.first else self.result(low - self.base, n)
        self.moving = self.wire.copy(src, self.result(low - self.base, n), flip(self.c, bit), landing=self.result(there - self.base, n)).start()
        self.first = False
        self.plan.later(self.plan.ship(road("c", bit, n * self.rows_us)), self.take_back)

    def take_back(self):
        self.moving.arrive()
        self.give_back()


def norm_rows(v):
    cen = v - jnp.mean(v, axis=-1, keepdims=True)
    rstd = lax.rsqrt(jnp.mean(cen * cen, axis=-1, keepdims=True) + EPS)
    return cen * rstd, rstd


def norm_back(grad, hat, rstd, gain):
    scaled = grad * gain
    return rstd * (scaled - jnp.mean(scaled, axis=-1, keepdims=True) - hat * jnp.mean(scaled * hat, axis=-1, keepdims=True))


def split3(v):
    hi = v.astype(BF).astype(F32)
    mid = (v - hi).astype(BF).astype(F32)
    return hi, mid, v - hi - mid


def layer(cfg, *refs):
    nc, nf, p, plans = cfg["nc"], cfg["nf"], cfg["p"], cfg["plans"]
    names = cfg["names"]
    R = dict(zip(names, refs, strict=True))
    x, cot, vec, lens = R["x"], R["cot"], R["vec"], R["lens"]
    wq_s, wo_s, wu_s, wd_s = R["wq_s"], R["wo_s"], R["wu_s"], R["wd_s"]
    wl, wo, wu, wd = R["wl"], R["wo"], R["wu"], R["wd"]
    vsum, bu = R["vsum"], R["bu"]
    xg, h1g, qp, kp, vp, of = R["xg"], R["h1g"], R["qp"], R["kp"], R["vp"], R["of"]
    omsg, oin, o2, res, h2, gb, gh = R["omsg"], R["oin"], R["o2"], R["res"], R["h2"], R["gb"], R["gh"]
    c, f = lax.axis_index("ctx"), lax.axis_index("fsdp")
    qs = nc // GROUPS
    g, m = c // qs, c % qs
    rows, D = x.shape
    T = rows // 2
    FF = wu.shape[1]
    core = c % 2
    sib = flip(c, 1)
    top = g // 4
    gq = g % 4
    odd = (gq % 2) == 1
    gf = flip(g, 4)
    far = flip(c, nc // 2)
    NQ = GROUPS * T
    NK = NQ * qs
    lsem = R["lsem"]
    wire = Wire(R["send"], R["recv"], f)

    done = set()

    def ready(i):
        if i not in done:
            loads[i].wait()
            done.add(i)

    lane = lax.broadcasted_iota(jnp.int32, (T, 128), 1)
    low = lane < HDIM

    off = (3 * (gq // 2) + gq % 2) * 128
    loads = []

    def load(src, dst):
        cp = pltpu.make_async_copy(src, dst, lsem.at[len(loads)])
        cp.start()
        loads.append(cp)

    nq = wq_s.shape[0]
    wcols = [span(i * D + off, 256, 128) for i in range(3)]
    for i in range(3):
        load(wq_s.at[:, wcols[i]], wl.at[span(f * nq, nq), i * 256 : (i + 1) * 256])
    for s, w in ((wo_s, wo), (wu_s, wu), (wd_s, wd)):
        load(s, w.at[span(f * s.shape[0], s.shape[0])])

    barrier = pltpu.get_barrier_semaphore()
    mates = [(((g + k) % GROUPS) * qs + m, f) for k in range(1, GROUPS)]
    mates += [(g * qs + (m + k) % qs, f) for k in range(1, qs)]
    mates += [(c, (f + k) % nf) for k in range(1, nf)]
    for mate in mates:
        pl.semaphore_signal(barrier, inc=1, device_id=mate, device_id_type=MESH)
    pl.semaphore_wait(barrier, len(mates))

    own_rows, other_rows = span(top * T, T), span((1 - top) * T, T)
    to_far = wire.copy(x.at[other_rows], xg.at[g], far, landing=xg.at[gf]).start()
    near = [(top * 4 + (gq + k) % 4, top * 4 + (gq + 4 - k) % 4) for k in (1, 2, 3)]
    own_out = [wire.copy(x.at[own_rows], xg.at[g], t * qs + m, landing=xg.at[s]).start() for t, s in near]
    far_out = [wire.copy(xg.at[gf], xg.at[gf], t * qs + m, landing=xg.at[flip(s, 4)]) for t, s in near]
    wq_out, vec_out = [], []
    for d in range(1, nf):
        fs = (f + nf - d) % nf
        vec_out.append(wire.copy(vec, R["vin"].at[f], c, (f + d) % nf, landing=R["vin"].at[fs]).start())
        for i in range(3):
            cols = slice(i * 256, (i + 1) * 256)
            wq_out.append(wire.copy(wq_s.at[:, wcols[i]], wl.at[span(f * nq, nq), cols], c, (f + d) % nf,
                                    landing=wl.at[span(fs * nq, nq), cols]).start())
    weights = [Gather(wire, c, f, nf, n, s, w) for n, s, w in ((p, wo_s, wo), (min(p, 4), wu_s, wu), (min(p, 4), wd_s, wd))]
    for w in weights:
        w.begin()
    to_far.arrive()
    for copy in far_out:
        copy.start()
    xg[g] = x[own_rows, :]
    vin = R["vin"]
    vin[f] = vec[...]
    for copy in vec_out:
        copy.arrive()
    vsum[...] = jnp.concatenate([vin[j].astype(F32) for j in range(nf)], axis=1)
    nv = vec.shape[1]
    bu[...] = jnp.concatenate([vsum[8 + i : 9 + i, j * nv : (j + 1) * nv] for j in range(nf) for i in range(FF // D)], axis=1)
    for mb in range(2):
        pos = c * T + lax.broadcasted_iota(jnp.int32, (T, D), 0)
        live = pos < lens[mb]
        gb[mb * T : (mb + 1) * T, :] = jnp.where(live, cot[mb * T : (mb + 1) * T, :].astype(F32), 0.0).astype(BF)
    hd = D // 2
    mine, theirs = span(core * hd, hd, 128), span((1 - core) * hd, hd, 128)
    gh[0:rows, :] = gb[:, mine]
    lower, upper = slice(0, rows), slice(rows, 2 * rows)
    g_out = wire.copy(gb.at[:, theirs], gh.at[upper], sib).start()

    for i in range(3):
        ready(i)
    for copy in wq_out:
        copy.arrive()
    length = jnp.where(top == 0, lens[0], lens[1])
    kaug_hi = jnp.where((lane >= 64) & (lane < 68), 1.0, 0.0)
    kaug_lo = jnp.where(lane < 4, 1.0, 0.0)
    vaug_hi = jnp.where((lane >= 64) & (lane < 67), 1.0, 0.0)
    vaug_lo = jnp.where(lane < 3, 1.0, 0.0)
    one_hi, one_lo = jnp.where(lane == 64, 1.0, 0.0), jnp.where(lane == 0, 1.0, 0.0)
    bias_q = vsum[2:3, span(off, 256, 128)]
    bias_v = vsum[3:4, span(off, 256, 128)]

    def pick(t0, t1):
        return jnp.where(odd, t1, t0), jnp.where(odd, pltpu.roll(t0, HDIM, 1), t1)

    def project(s):
        hat, _ = norm_rows(xg[s].astype(F32))
        h1 = (hat * vsum[0:1, :] + vsum[1:2, :]).astype(BF)
        qrows = span(s * T, T, 128)
        krows = span((m * GROUPS + s) * T, T, 128)
        h1g[qrows, :] = h1
        y = dot_nn(h1, wl[...])
        q = y[:, 0:256] + bias_q
        v = y[:, 512:768] + bias_v
        qa, qc = pick(q[:, 0:128], q[:, 128:256])
        ka, kc = pick(y[:, 256:384], y[:, 384:512])
        va, vc = pick(v[:, 0:128], v[:, 128:256])
        pos = (s * qs + m) * T + lax.broadcasted_iota(jnp.int32, (T, 128), 0)
        bias = jnp.where(pos < length, 0.0, -1e30)
        k_hi = jnp.where(lane == 64, bias, kaug_hi)
        k_lo = jnp.where(lane == 0, bias, kaug_lo)
        qa, qc = qa.astype(BF).astype(F32) * 0.125, qc.astype(BF).astype(F32) * 0.125
        qp[0, qrows, :] = jnp.where(low, qa, one_hi).astype(BF)
        qp[1, qrows, :] = jnp.where(low, one_lo, qa).astype(BF)
        qp[2, qrows, :] = jnp.where(low, qc, one_hi).astype(BF)
        kp[0, krows, :] = jnp.where(low, ka, k_hi).astype(BF)
        kp[1, krows, :] = jnp.where(low, k_lo, ka).astype(BF)
        kp[2, krows, :] = jnp.where(low, kc, k_hi).astype(BF)
        vp[0, krows, :] = jnp.where(low, va, vaug_hi).astype(BF)
        vp[1, krows, :] = jnp.where(low, vaug_lo, va).astype(BF)
        vp[2, krows, :] = jnp.where(low, vc, vaug_hi).astype(BF)

    def share(first):
        out = []
        for j in range(1, qs):
            for ref in (kp, vp):
                at = lambda who: ref.at[:, span((who * GROUPS + first) * T, 4 * T, 128), :]
                out.append(wire.copy(at(m), at(m), g * qs + (m + j) % qs, landing=at((m + qs - j) % qs)).start())
        return out

    for copy in own_out:
        copy.arrive()
    pl.loop(0, 4)(lambda i: project(top * 4 + i))
    shares = share(top * 4)
    for copy in far_out:
        copy.arrive()
    pl.loop(0, 4)(lambda i: project((1 - top) * 4 + i))
    shares += share((1 - top) * 4)
    weights[0].spread()
    weights[1].spread()
    for copy in shares:
        copy.arrive()
    weights[2].spread()

    tq = cfg["tq"]
    lane_q = lax.broadcasted_iota(jnp.int32, (tq, 128), 1)

    def attend(h):
        base = 0 if h == 1 else HDIM

        @pl.loop(0, NQ // tq)
        def _(i):
            at = span(i * tq, tq, 128)
            q = qp[h, at, :]
            s = dot_nt(q, kp[h])
            peak = jnp.max(s, axis=1, keepdims=True)
            e = jnp.exp(s - peak).astype(BF)
            o = dot_nn(e, vp[h])
            l = o[:, base : base + 1]
            of[h, at, :] = o / l
            a, b, d = split3(-(peak + jnp.log(l)))
            q = q.astype(F32)
            q = jnp.where(lane_q == base + 1, a, jnp.where(lane_q == base + 2, b, jnp.where(lane_q == base + 3, d, q)))
            qp[h, at, :] = q.astype(BF)

    def deal(msg, box, half):
        box[half, g] = msg[half, g]
        out = []
        for k in range(1, GROUPS):
            t, s = (g + k) % GROUPS, (g + GROUPS - k) % GROUPS
            out.append(wire.copy(msg.at[half, t], box.at[half, g], t * qs + m, landing=box.at[half, s]).start())
        return out

    attend(0)
    attend(1)

    @pl.loop(0, GROUPS)
    def _(s):
        at = span(s * T, T, 128)
        omsg[0, s] = jnp.where(low, of[0, at, :], of[1, at, :]).astype(BF)

    o_out = deal(omsg, oin, 0)
    weights[0].pass_on()
    attend(2)

    @pl.loop(0, GROUPS)
    def _(s):
        omsg[1, s] = of[2, span(s * T, T, 128), :].astype(BF)

    o_out += deal(omsg, oin, 1)
    weights[1].pass_on()
    weights[2].pass_on()
    for copy in o_out:
        copy.arrive()

    def tiles(jp):
        return [slice((3 * jp + i) * 128, (3 * jp + i + 1) * 128) for i in range(3)]

    for mb in range(2):
        for jp in range(2):
            g0 = 4 * mb + 2 * jp
            at = slice(mb * T, (mb + 1) * T)
            t0, t1, t2 = tiles(jp)
            o2[at, t0] = oin[0, g0]
            o2[at, t1] = jnp.where(low, oin[1, g0].astype(F32), pltpu.roll(oin[1, g0 + 1].astype(F32), HDIM, 1)).astype(BF)
            o2[at, t2] = oin[0, g0 + 1]
    o_pair = wire.copy(o2.at[lower], o2.at[upper], sib).start()
    ready(3)
    weights[0].finish()
    res[...] = x[...].astype(F32) + dot_nn(o2[lower, :], wo[...]) + vsum[4:5, :]
    hat2, _ = norm_rows(res[...])
    h2[lower, :] = (hat2 * vsum[5:6, :] + vsum[6:7, :]).astype(BF)
    h_pair = wire.copy(h2.at[lower], h2.at[upper], sib).start()
    for i in (1, 2):
        ready(3 + i)
        weights[i].finish()

    a2, duh, dus, dbu, acc, dh2 = R["a2"], R["duh"], R["dus"], R["dbu"], R["acc"], R["dh2"]
    acc[...] = jnp.zeros_like(acc)
    dh2[...] = jnp.zeros_like(dh2)
    hf = FF // 2

    def hidden(which, keep):
        @pl.loop(0, hf // WIDE)
        def _(i):
            col = which * hf + i * WIDE
            cols = span(col, WIDE, 128)
            u = dot_nn(h2[lower, :], wu[:, cols]) + bu[:, cols]
            phi = 0.5 + 0.5 * lax.erf(u * 0.7071067811865476)
            a = (u * phi).astype(BF)
            a2[lower, cols] = a
            da = dot_nt(gb[...], wd[span(col, WIDE, 128), :])
            slope = phi + u * (0.3989422804014327 * jnp.exp(-0.5 * u * u))
            du = (da * slope).astype(BF)
            keep[0:rows, span(i * WIDE, WIDE, 128)] = du
            dbu[:, cols] = jnp.sum(du.astype(F32), axis=0, keepdims=True)
            acc[...] += dot_nn(a, wd[span(col, WIDE, 128), :])
            dh2[...] += dot_nt(du, wu[:, cols])

    hidden(1 - core, dus)
    du_pair = wire.copy(dus, duh.at[upper], sib).start()
    half_cols = lambda which: span(which * hf, hf, 128)
    a_pair = [wire.copy(a2.at[lower, half_cols(1 - core)], a2.at[upper, half_cols(1 - core)], sib, landing=a2.at[upper, half_cols(core)]).start()]
    hidden(core, duh)
    a_pair.append(wire.copy(a2.at[lower, half_cols(core)], a2.at[upper, half_cols(core)], sib, landing=a2.at[upper, half_cols(1 - core)]).start())
    R["out"][...] = (res[...] + acc[...] + vsum[7:8, :]).astype(BF)
    plan = Planner()
    a_here = plan.ship({"core": 5.0})
    dr, dbh, dbs, dmsg, doin = R["dr"], R["dbh"], R["dbs"], omsg, R["doin"]
    dvb = R["dvb"]
    gd, gu, go, gqr = wd.at[:, 0:hd], wu.at[:, 0:hf], wo.at[:, 0:hd], wu.at[:, hf : hf + D]

    def residual_back():
        hat2, rstd2 = norm_rows(res[...])
        dvb[0, 5:6, :] = jnp.sum(dh2[...] * hat2, axis=0, keepdims=True)
        dvb[0, 6:7, :] = jnp.sum(dh2[...], axis=0, keepdims=True)
        dr[...] = gb[...].astype(F32) + norm_back(dh2[...], hat2, rstd2, vsum[5:6, :])
        db = dr[...].astype(BF)
        dbs[...] = db
        dvb[0, 4:5, :] = jnp.sum(db.astype(F32), axis=0, keepdims=True)
        dvb[0, 7:8, :] = jnp.sum(gb[...].astype(F32), axis=0, keepdims=True)
        dbh[0:rows, :] = dbs[:, mine]
        db_pair = wire.copy(dbs.at[:, theirs], dbh.at[upper], sib).start()
        acc[...] = dot_nt(db, wo[...])
        wire.drain(o_out)
        for t in range(GROUPS):
            mb, jj = t // 4, t % 4
            at = slice(mb * T, (mb + 1) * T)
            t0, t1, t2 = tiles(jj // 2)
            dmsg[0, t] = acc[at, t2 if jj % 2 else t0].astype(BF)
            single = acc[at, t1]
            dmsg[1, t] = (pltpu.roll(single, HDIM, 1) if jj % 2 else single).astype(BF)
        do_out = [deal(dmsg, doin, 0), deal(dmsg, doin, 1)]
        load = {"x": 2.7, "z": 4.0, "mid": 5.4}
        here = [plan.ship(load), plan.ship(load)]
        for w in weights:
            for copies in [w.a] + w.b + w.z:
                wire.drain(copies)
        wire.drain(far_out)
        return db_pair, do_out, here

    db_pair, do_out, do_here = plan.compute(2.0, residual_back)

    def shard(ref, half, c0, c1, lead=()):
        return lambda lo, n: ref.at[lead + (span(lo, n), span(core * half + c0, c1 - c0, 128))]

    lone = []

    def sibling(ref, half, c0, c1):
        def go():
            at = lambda which: ref.at[:, span(which * half + c0, c1 - c0, 128)]
            copy = wire.copy(at(core), at(core), sib, landing=at(1 - core)).start()
            plan.later(plan.ship({"core": 1.0}), copy.arrive)
        return go

    def reduction(k, j, grad, ref, half, c0, c1):
        boxes = [R[f"box_{k}{j}{i}"] for i in range(len(plans[k]))]
        Reduce(wire, plan, c, f, nf, grad.at[:, c0:c1], boxes, plans[k], shard(ref, half, c0, c1), sibling(ref, half, c0, c1),
               lsem.at[7 + len(lone)]).send()
        lone.append(k)

    def down_grads():
        for copy in a_pair:
            copy.arrive()
        g_out.arrive()

        @pl.loop(0, FF // WIDE)
        def _(i):
            at = span(i * WIDE, WIDE, 128)
            wd[at, 0:hd] = dot_tn(a2[:, at], gh[...]).astype(BF)

        for j, (c0, c1) in enumerate(cfg["cuts"]["d"]):
            reduction("d", j, gd, R["fd"], hd, c0, c1)

    plan.compute(2.0, down_grads, a_here)

    def up_grads():
        h_pair.arrive()
        du_pair.arrive()
        for j, (c0, c1) in enumerate(cfg["cuts"]["u"]):
            wu[:, c0:c1] = dot_tn(h2[...], duh[:, c0:c1]).astype(BF)
            reduction("u", j, gu, R["fu"], hf, c0, c1)

    plan.compute(2.2, up_grads)

    def out_grads():
        o_pair.arrive()
        db_pair.arrive()
        wo[:, 0:hd] = dot_tn(o2[...], dbh[...]).astype(BF)
        for j, (c0, c1) in enumerate(cfg["cuts"]["o"]):
            reduction("o", j, go, R["fo"], hd, c0, c1)

    plan.compute(0.7, out_grads)

    dop, dka, dva, dkv, dkvin, dqkv = (R[k] for k in ("dop", "dka", "dva", "dkv", "dkvin", "dqkv"))
    dqa = of
    tb, kc = cfg["tb"], cfg["kc"]
    lane_b = lax.broadcasted_iota(jnp.int32, (tb, 128), 1)

    def prepare(h):
        half = 1 if h == 2 else 0
        base = 0 if h == 1 else HDIM

        @pl.loop(0, GROUPS)
        def _(s):
            at = span(s * T, T, 128)
            d = doin[half, s].astype(F32)
            d = jnp.where(low, 0.0, d) if h == 1 else jnp.where(low, d, 0.0)
            a, b, e = split3(-jnp.sum(d * of[h, at, :], axis=1, keepdims=True))
            d = jnp.where(lane == base, a, jnp.where(lane == base + 1, b, jnp.where(lane == base + 2, e, d)))
            dop[h, at, :] = d.astype(BF)

    def retrace(h, first, last):
        keep = (lambda v: jnp.where(lane_b < HDIM, 0.0, v)) if h == 1 else (lambda v: jnp.where(lane_b < HDIM, v, 0.0))
        if h != 1 and first == 0:
            dka[...] = jnp.zeros((NK, 128), F32)
            dva[...] = jnp.zeros((NK, 128), F32)

        @pl.loop(first, last)
        def _(i):
            at = span(i * tb, tb, 128)
            q, d = qp[h, at, :], dop[h, at, :]
            q0, d0 = keep(q.astype(F32)).astype(BF), keep(d.astype(F32)).astype(BF)
            dq = jnp.zeros((tb, 128), F32)
            for j in range(NK // kc):
                ks = slice(j * kc, (j + 1) * kc)
                k, v = kp[h, ks, :], vp[h, ks, :]
                pt = jnp.exp(dot_nt(k, q))
                ds = (pt * dot_nt(v, d)).astype(BF)
                dva[ks, :] += dot_nn(pt.astype(BF), d0)
                dka[ks, :] += dot_nn(ds, q0)
                dq = dq + dot_tn(ds, k)
            dqa[h, at, :] = dq * 0.125

    def trade(half):
        out = []
        for j in range(1, qs):
            part = (m + j) % qs

            @pl.loop(0, GROUPS)
            def _(s):
                at = span((part * GROUPS + s) * T, T, 128)
                to = span(s * T, T, 128)
                dkv[j - 1, 0, to, :] = dka[at, :].astype(BF)
                dkv[j - 1, 1, to, :] = dva[at, :].astype(BF)

            out.append(wire.copy(dkv.at[j - 1], dkvin.at[j - 1, half], g * qs + part).start())
        return out

    def place(half, base, at, tile):
        if half == 0:
            dqkv[at, base : base + 128] = jnp.where(odd, dqkv[at, base : base + 128].astype(F32), tile).astype(BF)
            dqkv[at, base + 128 : base + 256] = jnp.where(odd, tile, dqkv[at, base + 128 : base + 256].astype(F32)).astype(BF)
        else:
            turned = pltpu.roll(tile, HDIM, 1)
            dqkv[at, base : base + 128] = jnp.where(odd, turned, dqkv[at, base : base + 128].astype(F32)).astype(BF)
            dqkv[at, base + 128 : base + 256] = jnp.where(odd, dqkv[at, base + 128 : base + 256].astype(F32), tile).astype(BF)

    def settle_heads(half, trades):
        for copy in trades:
            copy.arrive()
        wire.drain(trades)
        pair = half == 0

        @pl.loop(0, GROUPS)
        def _(s):
            at = span(s * T, T, 128)
            mine_at = span((m * GROUPS + s) * T, T, 128)
            if pair:
                tile = jnp.where(low, dqa[0, at, :], dqa[1, at, :])
            else:
                tile = jnp.where(low, dqa[2, at, :], 0.0)
            place(half, 0, at, tile)
            for which, acc_ref in ((0, dka), (1, dva)):
                tile = acc_ref[mine_at, :]
                for j in range(1, qs):
                    tile = tile + dkvin[j - 1, half, which, at, :].astype(F32)
                place(half, 256 * (which + 1), at, tile)

    def retrace_all(h):
        n = NQ // tb
        for first, last in ((0, n // 2), (n // 2, n)):
            plan.compute(3.2, lambda: retrace(h, first, last))

    def ready_pair():
        dqkv[...] = jnp.zeros_like(dqkv)
        for copy in do_out[0]:
            copy.arrive()
        prepare(0)
        prepare(1)

    def ready_single():
        for copy in do_out[1]:
            copy.arrive()
        prepare(2)

    plan.compute(1.9, ready_pair, do_here[0])
    retrace_all(0)
    retrace_all(1)
    trades = plan.compute(0.5, lambda: trade(0))
    pair_here = plan.ship({"core": 3.0})
    plan.compute(1.0, ready_single, do_here[1])
    plan.compute(1.0, lambda: settle_heads(0, trades), pair_here)
    retrace_all(2)
    trades = plan.compute(0.5, lambda: trade(1))
    plan.compute(1.0, lambda: settle_heads(1, trades), plan.ship({"core": 3.0}))

    dh1p, dh1in, dh1, farbox = xg, R["dh1in"], dh2, R["farbox"]
    gqh, box_c = wu.at[:, hf + D : hf + D + hd], dop

    def inputs_back():
        pl.loop(0, GROUPS)(lambda s: dh1p.__setitem__(s, dot_nt(dqkv[span(s * T, T, 128), :], wl[...]).astype(BF)))
        out = [wire.copy(dh1p.at[flip(t, 4)], dh1in.at[k, 1], t * qs + m).start() for k, (t, s) in enumerate(near)]
        out += [wire.copy(dh1p.at[t], dh1in.at[k, 0], t * qs + m).start() for k, (t, s) in enumerate(near)]
        return out

    dh_out = plan.compute(2.0, inputs_back)
    dh_here = [plan.ship({"x": 8.0, "z": 8.0}), plan.ship({"x": 8.0, "z": 8.0})]

    def qkv_grads():
        for i in range(0, D, 256):
            gqr[:, i : i + 256] = dot_tn(h1g[...], dqkv[:, i : i + 256]).astype(BF)
        return [
            wire.copy(gqr.at[:, span((1 - core) * hd + i * 128, 128, 128)], box_c.at[i, 0:D], sib).start() for i in range(hd // 128)
        ]

    gq_pair = plan.compute(2.0, qkv_grads)
    gq_here = plan.ship({"core": 2.0})

    def column_sums():
        colsum = lax.fori_loop(
            0, GROUPS, lambda i, t: t + jnp.sum(dqkv[span(i * T, T, 128), :].astype(F32), axis=0, keepdims=True), jnp.zeros((1, D), F32)
        )
        dvb[0, 2:4, :] = jnp.zeros((2, D), F32)
        dvb[0, 12:16, :] = jnp.zeros((4, D), F32)
        dvb[0, 2:3, span(off, 256, 128)] = colsum[:, 0:256]
        dvb[0, 3:4, span(off, 256, 128)] = colsum[:, 512:768]
        for i in range(FF // D):
            dvb[0, 8 + i : 9 + i, :] = dbu[0:1, i * D : (i + 1) * D]

    plan.compute(0.5, column_sums)
    fq = R["fq"]

    def spread_q():
        moves = [(2, [gq]), (1, [gq, flip(gq, 2)]), (0, None)]

        def go():
            bit, have = moves.pop(0)
            if bit:
                ref = lambda jj: fq.at[jj, :, span(core * hd, hd, 128)]
                mate = flip(c, bit * qs)
                copies = [wire.copy(ref(j), ref(j), mate, landing=ref(flip(j, bit))).start() for j in have]
                us = len(have) * fq.shape[1] * hd * 4 / 98e3
            else:
                at = lambda which: fq.at[:, :, span(which * hd, hd, 128)]
                copies = [wire.copy(at(core), at(core), sib, landing=at(1 - core)).start()]
                us = 12.0

            def come():
                for copy in copies:
                    copy.arrive()
                if moves:
                    go()

            plan.later(plan.ship(road("c", 2 * bit if bit else 1, us)), come)

        go()

    def sum_q():
        for copy in gq_pair:
            copy.arrive()
        for i in range(hd // 128):
            at = slice(i * 128, (i + 1) * 128)
            gqh[:, at] = (gqr[:, span(core * hd + i * 128, 128, 128)].astype(F32) + box_c[i, 0:D].astype(F32)).astype(BF)
        Reduce(wire, plan, c, f, nf, gqh, [R[f"box_q0{i}"] for i in range(len(plans["q"]))], plans["q"],
               shard(fq, hd, 0, hd, (gq,)), spread_q, lsem.at[6]).send()

    plan.compute(0.5, sum_q, gq_here)

    def total_of(which, block):
        s = dh1p[block].astype(F32)
        for k in range(3):
            s = s + dh1in[k, which].astype(F32)
        return s

    def far_total():
        for copy in dh_out[:3]:
            copy.arrive()
        wire.drain([g_out])
        gb[0:T, :] = total_of(1, gf).astype(BF)
        return wire.copy(gb.at[0:T], farbox, far).start()

    far_back = plan.compute(0.5, far_total, dh_here[0])
    far_here = plan.ship({"z": 4.0, "mid": 8.0})

    def near_total():
        for copy in dh_out[3:]:
            copy.arrive()
        dh1[own_rows, :] = total_of(0, g)

    plan.compute(0.5, near_total, dh_here[1])
    dvin = R["dvin"]
    bits = [("c", 1 << b) for b in range(nc.bit_length() - 1)] + [("f", 1 << b) for b in range(nf.bit_length() - 1)]

    def vectors(i=0):
        if i == len(bits):
            final, own = dvb[i], jnp.zeros((16, nv), F32)
            for j in range(nf):
                own = jnp.where(f == j, final[:, j * nv : (j + 1) * nv], own)
            for r in range(FF // D):
                for j in range(nf):
                    flat = (j * (FF // D) + r) * nv
                    piece = final[8 + flat // D : 9 + flat // D, flat % D : flat % D + nv]
                    R["dvec"][8 + r : 9 + r, :] = piece if j == 0 else jnp.where(f == j, piece, R["dvec"][8 + r : 9 + r, :])
            R["dvec"][0:8, :] = own[0:8]
            R["dvec"][12:16, :] = own[12:16]
            return
        axis, bit = bits[i]
        peer = (c, flip(f, bit)) if axis == "f" else (flip(c, bit), f)
        moved = wire.copy(dvb.at[i], dvin.at[i], *peer).start()

        def come():
            moved.arrive()
            dvb[i + 1] = dvb[i] + dvin[i]
            vectors(i + 1)

        plan.later(plan.ship(road(axis, bit, 1.0)), come)

    def finish_inputs():
        far_back.arrive()
        dh1[other_rows, :] = farbox[...].astype(F32)
        hat1, rstd1 = norm_rows(x[...].astype(F32))
        dvb[0, 0:1, :] = jnp.sum(dh1[...] * hat1, axis=0, keepdims=True)
        dvb[0, 1:2, :] = jnp.sum(dh1[...], axis=0, keepdims=True)
        vectors()
        R["gin"][...] = (dr[...] + norm_back(dh1[...], hat1, rstd1, vsum[0:1, :])).astype(BF)

    plan.compute(1.7, finish_inputs, far_here)
    plan.finish()
    gq_o = R["gq"]
    nrow = fq.shape[1]
    step = next(n for n in (128, 96, 64, 48, 32, 16) if nrow % n == 0)

    @pl.loop(0, nrow // step)
    def _(i):
        at = span(i * step, step)
        for t in range(3):
            for a in range(2):
                base, src = t * D + a * 384, 256 * t
                gq_o[at, base : base + 128] = fq[2 * a, at, src : src + 128]
                shared = fq[2 * a, at, src + 128 : src + 256].astype(F32) + fq[2 * a + 1, at, src : src + 128].astype(F32)
                gq_o[at, base + 128 : base + 256] = shared.astype(BF)
                gq_o[at, base + 256 : base + 384] = fq[2 * a + 1, at, src + 128 : src + 256]

    wire.drain()


def call(nc, nf, x, cot, vec, lens, wq, wo, wu, wd):
    qs = nc // GROUPS
    R, D = x.shape
    T, FF = R // 2, wu.shape[1]
    NQ, NK = GROUPS * T, GROUPS * T * qs
    hd, hf = D // 2, FF // 2
    p = next(p for p in (8, 4, 2) if nc % p == 0 and all(w.shape[0] % (16 * p) == 0 for w in (wo, wu, wd)))
    fbits = [("f", 1 << b) for b in reversed(range(nf.bit_length() - 1))]
    cbits = [("c", 1 << b) for b in range(1, nc.bit_length() - 1)]
    qbits = [("c", 1 << b) for b in range(1, qs.bit_length() - 1)] + [("c", nc // 2)]
    plans = {"d": reduce_plan(FF, fbits + cbits), "u": reduce_plan(D, fbits + cbits), "o": reduce_plan(D, fbits + cbits),
             "q": reduce_plan(D, fbits + qbits)}
    sds, dma = jax.ShapeDtypeStruct, pltpu.SemaphoreType.DMA
    any_, vm, sm = (pl.BlockSpec(memory_space=s) for s in (pl.ANY, pltpu.VMEM, pltpu.SMEM))
    ins = ["x", "cot", "vec", "lens", "wq_s", "wo_s", "wu_s", "wd_s"]
    outs = {"out": sds((R, D), BF), "gin": sds((R, D), BF), "dvec": sds((16, D // nf), F32), "gq": sds((D // nf, 3 * D), BF),
            "fo": sds((D // nf, D), BF), "fu": sds((D // nf, FF), BF), "fd": sds((FF // nf, D), BF)}
    nb = nc.bit_length() + nf.bit_length() - 2
    b, s = (lambda *shape: pltpu.VMEM(shape, BF)), (lambda *shape: pltpu.VMEM(shape, F32))
    scratch = {
        "wl": b(D, D), "wo": b(D, D), "wu": b(D, FF), "wd": b(FF, D), "vsum": s(16, D), "bu": s(1, FF), "vin": b(nf, 16, D // nf),
        "xg": b(GROUPS, T, D), "h1g": b(NQ, D), "qp": b(3, NQ, 128), "kp": b(3, NK, 128), "vp": b(3, NK, 128), "of": s(3, NQ, 128),
        "omsg": b(2, GROUPS, T, 128), "oin": b(2, GROUPS, T, 128), "o2": b(2 * R, D), "res": s(R, D), "h2": b(2 * R, D), "gb": b(R, D),
        "gh": b(2 * R, hd), "a2": b(2 * R, FF), "duh": b(2 * R, hf), "dus": b(R, hf), "dbu": s(1, FF), "acc": s(R, D), "dh2": s(R, D),
        "dr": s(R, D), "dbh": b(2 * R, hd), "dbs": b(R, D), "doin": b(2, GROUPS, T, 128),
        "dop": b(3, NQ, 128), "dka": s(NK, 128), "dva": s(NK, 128),
        "dkv": b(qs - 1, 2, NQ, 128), "dkvin": b(qs - 1, 2, 2, NQ, 128), "dqkv": b(NQ, D),
        "dh1in": b(3, 2, T, D), "farbox": b(T, D),
        "dvb": s(nb + 1, 16, D), "dvin": s(nb, 16, D),
        "fq": b(4, D // nf, D),
        "lsem": dma((16,)), "send": dma((400,)), "recv": dma((400,)),
    }
    cuts = {"d": [(i, i + 128) for i in range(0, hd, 128)], "u": [(i, i + 512) for i in range(0, hf, 512)], "o": [(0, hd)], "q": [(0, hd)]}
    for k in cuts:
        for j, (c0, c1) in enumerate(cuts[k]):
            for i, (_, _, _, n) in enumerate(plans[k]):
                scratch[f"box_{k}{j}{i}"] = b(n, c1 - c0)
    cfg = dict(nc=nc, nf=nf, p=p, plans=plans, names=ins + list(outs) + list(scratch), cuts=cuts, tq=128, tb=256, kc=512)
    return pl.pallas_call(
        functools.partial(layer, cfg),
        out_shape=list(outs.values()),
        in_specs=[vm, vm, vm, sm, any_, any_, any_, any_],
        out_specs=[vm, vm, vm, vm, any_, any_, any_],
        scratch_shapes=list(scratch.values()),
        compiler_params=pltpu.CompilerParams(collective_id=0, has_side_effects=True, vmem_limit_bytes=62_464 * 1024),
    )(x, cot, vec, lens, wq, wo, wu, wd)


def body(inputs, cotangent, lengths, g1, b1, w_qkv, bias_q, bias_v, w_out, bias_out, g2, b2, w_up, bias_up, w_down, bias_down, nc, nf):
    MB, _, T, D = inputs.shape
    n = g1.shape[0]
    small, at, flat = [g1, b1, bias_q, bias_v, bias_out, g2, b2, bias_down, bias_up], 0, 0
    for v in small:
        flat = flat + lax.pad(v, jnp.zeros((), BF), ((at, 16 * n - at - v.shape[0], 0),))
        at += v.shape[0]
    vec = flat.reshape(16, n)
    out, gin, dvec, fq, fo, fu, fd = call(nc, nf, inputs.reshape(MB * T, D), cotangent.reshape(MB * T, D), vec, lengths[:, 0],
                                          w_qkv, w_out, w_up, w_down)
    grads = [v.astype(F32) for v in (fq, fo, fu, fd)]
    shape = (MB, 1, T, D)
    row = lambda i: dvec[i]
    return (out.reshape(shape), gin.reshape(shape), row(0), row(1), grads[0], row(2), row(3), grads[1], row(4),
            row(5), row(6), grads[2], dvec[8:12].reshape(-1), grads[3], row(7))


def solution(mesh):
    nc, nf = mesh.shape["ctx"], mesh.shape["fsdp"]
    act = P(None, "fsdp", "ctx", None)
    one, two = P("fsdp"), P("fsdp", None)
    return jax.shard_map(
        functools.partial(body, nc=nc, nf=nf),
        mesh=mesh,
        in_specs=(act, act, P(None, "fsdp"), one, one, two, one, one, two, one, one, one, two, one, two, one),
        out_specs=(act, act, one, one, two, one, one, two, one, one, one, two, one, two, one),
        check_vma=False,
    )
```
